256 devices in a mesh: ctx: 32 (over y, x, core), head: 8 (over z).
Axes of the slice: x: 4, y: 4, z: 8, core: 2. Of those that a mesh axis runs over, the one named last changes fastest.
Arguments:
- queries: bfloat16 [32, 4096, 128], P('head', 'ctx'), may hold values from -6 to 6
- keys: bfloat16 [32, 4096, 128], P('head', 'ctx'), may hold values from -6 to 6
- values_in: bfloat16 [32, 4096, 128], P('head', 'ctx'), may hold values from -6 to 6
- out_grad: bfloat16 [32, 4096, 128], P('head', 'ctx'), may hold values from -1.5 to 1.5
- logged_keep_factor: float32 [32, 4096, 128], P('head', 'ctx'), may hold values from -0.75 to 0
- beta: float32 [32, 4096], P('head', 'ctx'), may hold values from 0.1 to 0.95
- conv_weight: float32 [4, 32, 128], P(None, 'head'), may hold values from -2 to 2
Outputs:
- query_grad: float32 [32, 4096, 128], P('head', 'ctx')
- input_grad: float32 [32, 4096, 128], P('head', 'ctx')
The draws below stay inside these ranges and needn't reach their ends.
All inputs are finite; a program needn't handle non-finite values.
Results may differ from the reference program's by a relative error of at most 0.0003.
Values may be sent and summed in bfloat16 or wider, within the bound.
A program may use at most 128 MiB of HBM per device.

```python
import math
import jax
import jax.numpy as jnp
from jax import lax

H = 32
DK = 128
CONV = 4
TOKENS = 4096


def draw_logged_keep_factor(key, part):
    keys_split = jax.random.split(key, 6)
    slow_share = 0.5
    slow = jax.random.uniform(keys_split[0], (H, 1, DK), jnp.float32) < slow_share
    slow_rate = jnp.exp(jax.random.uniform(keys_split[1], (H, 1, DK), jnp.float32, math.log(0.1), 0.0)) / TOKENS
    fast_rate = jnp.exp(jax.random.uniform(keys_split[2], (H, 1, DK), jnp.float32, math.log(1.0 / 50.0), math.log(1.0 / 30.0)))
    fading_speed = jnp.where(slow, slow_rate, fast_rate)
    rough_guess = jax.random.uniform(keys_split[3], (H, TOKENS, DK), jnp.float32, 0.5, 1.5)
    desired_agreement = jax.random.uniform(keys_split[4], (H, TOKENS, 1), jnp.float32) < 4.0 / TOKENS
    objective_scalar = jnp.log(jax.random.uniform(keys_split[5], (H, TOKENS, 1), jnp.float32, 0.5, 0.8))
    neighbour_span = jnp.where(desired_agreement, objective_scalar, 0.0)
    return (-fading_speed * rough_guess + neighbour_span).astype(jnp.float32)


def draw_keys(key, part):
    keys_split = jax.random.split(jax.random.fold_in(key, 17), 2)
    strong_count = max(DK // 8, 1)
    leak = math.sqrt(float(strong_count) / float(TOKENS))
    orders = jax.vmap(lambda single_key: jax.random.permutation(single_key, DK))(jax.random.split(keys_split[0], H))
    strong = (orders < strong_count)[:, None, :]
    entries = jax.random.normal(keys_split[1], (H, TOKENS, DK), jnp.float32)
    shaped = jnp.where(strong, entries, leak * entries)
    return jnp.clip(shaped, -6.0, 6.0).astype(jnp.bfloat16)


def block_scale(rng, dims, cuts, least, high):
    level, own = 1.0, jax.random.fold_in(rng, 6)
    for dim, parts in cuts:
        draws = jnp.exp(jax.random.uniform(jax.random.fold_in(own, dim), (parts,), jnp.float32, least / len(cuts), high / len(cuts)))
        level = level * jnp.repeat(draws, dims[dim] // parts).reshape([-1 if axis == dim else 1 for axis in range(len(dims))])
    return level


def centred(key, extent, scale, limit, cuts=(), held_as=jnp.bfloat16):
    values = jax.random.normal(key, extent, jnp.float32) * scale
    if len(cuts) > 0:
        values = block_scale(key, extent, cuts, -0.22, 0.18) * values
    return jnp.clip(values, min=-limit, max=limit).astype(held_as)


def setup_inputs(seed: int = 0) -> dict:
    key_of = jax.random.split(jax.random.key(seed), 8)
    queries = centred(key_of[0], (H, TOKENS, DK), 1.0, 6.0, ((0, 8), (1, 32)))
    keys = draw_keys(jax.random.fold_in(key_of[7], 71), 0)
    values_in = centred(key_of[2], (H, TOKENS, DK), 1.0, 6.0, ((0, 8), (1, 32)))
    out_grad = centred(key_of[3], (H, TOKENS, DK), 0.25, 1.5, ((0, 8), (1, 32)))
    logged_keep_factor = draw_logged_keep_factor(jax.random.fold_in(key_of[7], 71), 0)
    beta = jnp.clip(0.1 + 0.84999999 * jax.random.uniform(key_of[5], (H, TOKENS), jnp.float32) ** block_scale(key_of[5], (H, TOKENS), ((0, 8), (1, 32)), -0.2, 0.2), 0.1, 0.95)
    conv_weight = centred(key_of[6], (CONV, H, DK), 0.5, 2.0, ((1, 8),), jnp.float32)
    return dict(queries=queries, keys=keys, values_in=values_in, out_grad=out_grad, logged_keep_factor=logged_keep_factor, beta=beta, conv_weight=conv_weight)


highest = lax.Precision.HIGHEST

def normalize(array):
    scaled = array.astype(jnp.float32)
    return scaled * lax.rsqrt(lax.optimization_barrier(jnp.sum(scaled * scaled, axis=-1, keepdims=True)) + 1e-06)

def by_token(array):
    return jnp.swapaxes(array, 0, 1)

def reference(queries, keys, values_in, out_grad, logged_keep_factor, beta, conv_weight):
    query_unit = normalize(queries)
    key_unit = normalize(keys)
    conv_taps = conv_weight.shape[0]
    token_count = values_in.shape[1]
    inputs_f = values_in.astype(jnp.float32)
    padded = jnp.pad(inputs_f, ((0, 0), (conv_taps - 1, 0), (0, 0)))
    pre_act = conv_weight[0][:, None, :] * padded[:, conv_taps - 1:conv_taps - 1 + token_count, :]
    for tap in range(1, conv_taps):
        pre_act = pre_act + conv_weight[tap][:, None, :] * padded[:, conv_taps - 1 - tap:conv_taps - 1 - tap + token_count, :]
    sigmoid_pre = jax.nn.sigmoid(pre_act)
    value = pre_act * sigmoid_pre
    decay = jnp.exp(logged_keep_factor)
    out_f = out_grad.astype(jnp.float32)
    head_count, key_width = (queries.shape[0], queries.shape[2])
    initial = jnp.zeros((head_count, key_width, key_width), jnp.float32)

    def forward_step(state, sliced):
        key_now, value_now, decay_now, beta_now, out_now = sliced
        decayed = decay_now[:, :, None] * state
        recalled = jnp.einsum('hc,hcd->hd', key_now, decayed, precision=highest)
        state = decayed + (beta_now[:, None] * key_now)[:, :, None] * (value_now - recalled)[:, None, :]
        return (state, jnp.einsum('hcd,hd->hc', state, out_now, precision=highest))
    _, query_grad = lax.scan(forward_step, initial, (by_token(key_unit), by_token(value), by_token(decay), beta.T, by_token(out_f)))

    def backward_step(carry, sliced):
        query_now, key_now, decay_now, beta_now, out_now = sliced
        gradient = carry + query_now[:, :, None] * out_now[:, None, :]
        value_now = beta_now[:, None] * jnp.einsum('hcd,hc->hd', gradient, key_now, precision=highest)
        carry = decay_now[:, :, None] * (gradient - key_now[:, :, None] * value_now[:, None, :])
        return (carry, value_now)
    _, value_grad = lax.scan(backward_step, initial, (by_token(query_unit), by_token(key_unit), by_token(decay), beta.T, by_token(out_f)), reverse=True)
    value_grad = by_token(value_grad)
    pre_grad = value_grad * sigmoid_pre * (1.0 + pre_act * (1.0 - sigmoid_pre))
    extended = jnp.pad(pre_grad, ((0, 0), (0, conv_taps - 1), (0, 0)))
    input_grad = conv_weight[0][:, None, :] * extended[:, 0:token_count, :]
    for tap in range(1, conv_taps):
        input_grad = input_grad + conv_weight[tap][:, None, :] * extended[:, tap:tap + token_count, :]
    return (by_token(query_grad), input_grad)
```

```python
import jax
import jax.numpy as jnp
from jax import lax
from jax.experimental import pallas as pl
from jax.experimental.pallas import tpu as pltpu
from jax.sharding import PartitionSpec as P

MESH = pl.DeviceIdType.MESH
F32 = jnp.float32
BF16 = jnp.bfloat16
HEADS = 4
N = 128
SIDE = 4
RING = 32


def split(a):
    high = a.astype(BF16)
    return high, (a - high.astype(F32)).astype(BF16)


def left(a):
    return jnp.concatenate(split(a), axis=1)


def right(*arrays):
    row = jnp.concatenate([part for a in arrays for part in split(a)], axis=1)
    return jnp.concatenate([row, row], axis=0)


def right_t(a):
    high, low = split(a)
    return jnp.concatenate(
        [jnp.concatenate([high, high], axis=1), jnp.concatenate([low, low], axis=1)], axis=0
    )


def halves(wide):
    return [
        wide[:, 2 * N * i : 2 * N * i + N] + wide[:, 2 * N * i + N : 2 * N * (i + 1)]
        for i in range(wide.shape[1] // (2 * N))
    ]


def mm(a, *bs):
    out = halves(jnp.dot(left(a), right(*bs), preferred_element_type=F32))
    return out[0] if len(bs) == 1 else out


def mm_t(a, b):
    return halves(
        lax.dot_general(
            left(a), right_t(b), (((1,), (1,)), ((), ())), preferred_element_type=F32
        )
    )[0]


def mm_exact(a, b):
    return jnp.dot(left(a), jnp.concatenate([b, b], axis=0), preferred_element_type=F32)


def kernel(
    q_ref, k_ref, v_ref, o_ref, g_ref, beta_ref, w_ref, qg_ref, ig_ref,
    tail, halo_v, padded, dsig, loc, pair, chip, row, tot, above, pref, start, sends, back, states,
    xk, pl_mix, wt, lg, kgc, e0, e1, pg_first, pg_next, pg_pad,
    tail_s, tail_r, pair_s, pair_r, row_s, row_r, up_s, up_r, back_s, back_r, fwd_s, fwd_r, pg_s, pg_r,
):
    me = lax.axis_index("ctx")
    head = lax.axis_index("head")
    c = lax.rem(me, 2)
    x = lax.rem(me // 2, SIDE)
    y = me // (2 * SIDE)

    def at(yy, xx, cc):
        return ((yy * SIDE + xx) * 2 + cc, head)

    def place(v):
        return v * (2 * c - 1) + (SIDE - 1) * (1 - c)

    p, r = place(x), place(y)
    partner = at(y, x, 1 - c)
    following = (lax.rem(me + 1, RING), head)
    preceding = (lax.rem(me + RING - 1, RING), head)
    other_near = (lax.rem(me + 2 * c - 1 + RING, RING), head)

    barrier = pltpu.get_barrier_semaphore()
    greeted = [partner, other_near]
    greeted += [at(y, lax.rem(x + d, SIDE), c) for d in range(1, SIDE)]
    greeted += [at(lax.rem(y + d, SIDE), x, c) for d in range(1, SIDE)]
    for device in greeted:
        pl.semaphore_signal(barrier, inc=1, device_id=device, device_id_type=MESH)

    def remote(src, dst, send, recv, device):
        return pltpu.make_async_remote_copy(
            src_ref=src, dst_ref=dst, send_sem=send, recv_sem=recv,
            device_id=device, device_id_type=MESH,
        )

    tail[...] = v_ref[:, N - 16 :, :]
    pl.semaphore_wait(barrier, len(greeted))
    tail_copy = remote(tail, halo_v, tail_s, tail_r, following)
    tail_copy.start()

    t_id = lax.broadcasted_iota(jnp.int32, (N, N), 0)
    s_id = lax.broadcasted_iota(jnp.int32, (N, N), 1)
    lower_ones = jnp.where(t_id >= s_id, 1.0, 0.0).astype(BF16)
    eye = jnp.where(t_id == s_id, 1.0, 0.0).astype(F32)

    def block_mask(small, large):
        return (t_id // large == s_id // large) & (t_id // small > s_id // small)

    heads = range(HEADS)
    system, kd_all, ket_all, ke_all, kdt_all, rhs_all, qto_all, keep_all = [[] for _ in range(8)]
    for h in heads:
        q = q_ref[h].astype(F32)
        q = q * lax.rsqrt(jnp.sum(q * q, axis=1, keepdims=True) + 1e-6)
        k = k_ref[h].astype(F32)
        k = k * lax.rsqrt(jnp.sum(k * k, axis=1, keepdims=True) + 1e-6)
        g = g_ref[h]
        g_high = g.astype(BF16)
        rest = g - g_high.astype(F32)
        g_mid = rest.astype(BF16)
        g_low = (rest - g_mid.astype(F32)).astype(BF16)
        sums = jnp.dot(
            lower_ones, jnp.concatenate([g_high, g_mid, g_low], axis=1), preferred_element_type=F32
        )
        ld = sums[:, :N] + (sums[:, N : 2 * N] + sums[:, 2 * N :])
        middle = ld[N // 2 - 1 : N // 2, :]
        last = ld[N - 1 :, :]
        since = jnp.exp(ld - middle)
        until = jnp.exp(middle - ld)
        full = since * jnp.exp(middle)
        to_end = until * jnp.exp(last - middle)
        e1[h] = since
        e0[h] = full
        beta_row = beta_ref[h : h + 1, :]
        beta_col = jnp.sum(eye * beta_row, axis=1, keepdims=True)
        k_until = k * until
        kgc[h] = k_until
        kd = k * full
        ke = k * to_end
        ket_all.append(ke.T * beta_row)
        ke_all.append(ke * beta_col)
        kd_all.append(kd)
        kdt_all.append(kd.T)
        mix = mm_t(k * since, k_until)
        system.append(jnp.where(t_id > s_id, mix * beta_row, 0.0))
        upper = jnp.where(s_id >= t_id, mm_t(k_until, q * since), 0.0)
        rhs_all.append(beta_col * mm_exact(upper, o_ref[h]))
        qto_all.append(mm_exact((q * full).T, o_ref[h]))
        keep_all.append(jnp.exp(last))

    inverse = [eye - jnp.where(block_mask(1, 2), system[h], 0.0) for h in heads]
    for small in (2, 8, 32):
        mask = block_mask(small, 4 * small)
        for h in heads:
            m = mm(inverse[h], jnp.where(mask, system[h], 0.0))
            squared, applied = mm(m, m, inverse[h])
            z = inverse[h] - applied
            inverse[h] = z + mm(squared, z)

    tail_copy.wait_recv()
    for h in heads:
        padded[h, 8:, :] = v_ref[h].astype(F32)
        edge = halo_v[h].astype(F32)[8:, :]
        padded[h, :8, :] = jnp.where(me > 0, edge, 0.0)
        pre = w_ref[0, h : h + 1, :] * padded[h, 8:, :]
        for j in range(1, 4):
            pre = pre + w_ref[j, h : h + 1, :] * padded[h, 8 - j : 8 - j + N, :]
        sig = jax.nn.sigmoid(pre)
        dsig[h] = sig * (1.0 + pre * (1.0 - sig))
        value = pre * sig
        keys_x, values_x = mm(inverse[h], kd_all[h], value)
        keys_xt = mm_t(kdt_all[h], inverse[h])
        fwd_t, fwd_f = mm(ket_all[h], keys_x, values_x)
        bwd_t, bwd_f = mm(keys_xt, ke_all[h], rhs_all[h])
        keep = eye * keep_all[h]
        loc[h, 0, 0] = keep - fwd_t
        loc[h, 0, 1] = fwd_f
        loc[h, 1, 0] = keep - bwd_t
        loc[h, 1, 1] = qto_all[h] - bwd_f
        xk[h] = keys_x
        remote(loc.at[h, c], pair.at[h], pair_s.at[h], pair_r.at[h], partner).start()
        out_values = lax.dot_general(
            jnp.concatenate([o_ref[h], o_ref[h]], axis=1), jnp.concatenate(split(values_x), axis=1),
            (((1,), (1,)), ((), ())), preferred_element_type=F32,
        )
        pl_mix[h] = jnp.where(t_id >= s_id, out_values, 0.0) * beta_ref[h : h + 1, :]
        wt[h], lg[h] = mm(inverse[h].T, ke_all[h], rhs_all[h])

    for h in heads:
        remote(loc.at[h, c], pair.at[h], pair_s.at[h], pair_r.at[h], partner).wait_recv()
        g_chip, f_chip = mm(loc[h, 1 - c, 0], pair[h, 0], pair[h, 1])
        chip[h, 0] = g_chip
        chip[h, 1] = f_chip + loc[h, 1 - c, 1]

        @pl.when(x != h)
        def _():
            remote(chip.at[h], row.at[p], row_s.at[h], row_r.at[p], at(y, h, c)).start()

        @pl.when(x == h)
        def _():
            row[p] = chip[h]

    for d in range(1, SIDE):
        source = lax.rem(x + d, SIDE)
        slot = place(source)
        remote(chip.at[0], row.at[slot], row_s.at[0], row_r.at[slot], at(y, source, c)).wait_recv()
    p2, o2 = mm(row[1, 0], row[0, 0], row[0, 1])
    o2 = o2 + row[1, 1]
    q2, r2 = mm(row[3, 0], row[2, 0], row[2, 1])
    r2 = r2 + row[3, 1]
    tg, tf = mm(q2, p2, o2)
    tot[0] = tg
    tot[1] = tf + r2

    def up(kind, target):
        return remote(
            tot.at[kind], above.at[r, kind], up_s.at[target, kind], up_r.at[r, kind],
            at(place(target), x, c),
        )

    for target in range(1, SIDE):
        @pl.when(r < target)
        def _():
            up(1, target).start()

        @pl.when((r < target) & (r > 0))
        def _():
            up(0, target).start()

    p3, o3 = mm(row[2, 0], p2, o2)
    pref[0, 0] = row[0, 0]
    pref[0, 1] = row[0, 1]
    pref[1, 0] = p2
    pref[1, 1] = o2
    pref[2, 0] = p3
    pref[2, 1] = o3 + row[2, 1]

    def got(source, kind):
        remote(
            tot.at[kind], above.at[source, kind], up_s.at[1, kind], up_r.at[source, kind], partner
        ).wait_recv()

    start[...] = jnp.zeros((N, N), F32)

    @pl.when(r >= 1)
    def _():
        got(0, 1)
        start[...] = above[0, 1]

    for source in (1, 2):
        @pl.when(r > source)
        def _():
            got(source, 0)
            got(source, 1)
            start[...] = mm(above[source, 0], start[...]) + above[source, 1]

    for target in range(SIDE):
        if target == 0:
            sends[0] = start[...]
        else:
            sends[target] = mm(pref[target - 1, 0], start[...]) + pref[target - 1, 1]
        to = place(target)

        @pl.when(to != x)
        def _():
            remote(
                sends.at[target], back.at[x], back_s.at[target], back_r.at[x], at(y, to, c)
            ).start()

        @pl.when(to == x)
        def _():
            back[x] = sends[target]

    for h in heads:
        @pl.when(x != h)
        def _():
            remote(sends.at[0], back.at[h], back_s.at[0], back_r.at[h], partner).wait_recv()

        remote(back.at[h], states.at[1 - c, h], fwd_s.at[h], fwd_r.at[h], partner).start()
        states[1 - c, h] = mm(pair[h, 0], back[h]) + pair[h, 1]

    for h in heads:
        remote(back.at[h], states.at[c, h], fwd_s.at[h], fwd_r.at[h], partner).wait_recv()
        pg = (lg[h] + mm(wt[h], states[1, h])) * dsig[h]
        pg_pad[h, :N, :] = pg
        pg_first[h] = pg[:8, :]
    pg_copy = remote(pg_first, pg_next, pg_s, pg_r, preceding)
    pg_copy.start()
    for h in heads:
        state = states[0, h]
        reach = lax.dot_general(
            jnp.concatenate([o_ref[h], o_ref[h]], axis=1),
            jnp.concatenate(split(state), axis=1),
            (((1,), (1,)), ((), ())), preferred_element_type=F32,
        )
        mixed = mm_t(reach, xk[h])
        weights = pl_mix[h] - jnp.where(t_id >= s_id, mixed, 0.0) * beta_ref[h : h + 1, :]
        qg_ref[h] = e1[h] * mm(weights, kgc[h]) + e0[h] * reach

    pg_copy.wait_recv()
    for h in heads:
        pg_pad[h, N:, :] = jnp.where(me < RING - 1, pg_next[h], 0.0)
        grad = w_ref[0, h : h + 1, :] * pg_pad[h, :N, :]
        for j in range(1, 4):
            grad = grad + w_ref[j, h : h + 1, :] * pg_pad[h, j : j + N, :]
        ig_ref[h] = grad

    tail_copy.wait_send()
    pg_copy.wait_send()
    for h in heads:
        remote(loc.at[h, c], pair.at[h], pair_s.at[h], pair_r.at[h], partner).wait_send()
        remote(back.at[h], states.at[1 - c, h], fwd_s.at[h], fwd_r.at[h], partner).wait_send()

        @pl.when(x != h)
        def _():
            remote(chip.at[h], row.at[p], row_s.at[h], row_r.at[p], at(y, h, c)).wait_send()

    for target in range(1, SIDE):
        @pl.when(r < target)
        def _():
            up(1, target).wait_send()

        @pl.when((r < target) & (r > 0))
        def _():
            up(0, target).wait_send()

    for target in range(SIDE):
        @pl.when(place(target) != x)
        def _():
            remote(
                sends.at[target], back.at[x], back_s.at[target], back_r.at[x], at(y, x, c)
            ).wait_send()


def local(queries, keys, values_in, out_grad, logged_keep_factor, beta, conv_weight):
    vmem = pl.BlockSpec(memory_space=pltpu.VMEM)
    sem = pltpu.SemaphoreType.DMA
    square = lambda *lead: pltpu.VMEM((*lead, N, N), F32)
    out = jax.ShapeDtypeStruct((HEADS, N, N), F32)
    return pl.pallas_call(
        kernel,
        out_shape=(out, out),
        in_specs=[vmem] * 7,
        out_specs=(vmem, vmem),
        scratch_shapes=[
            pltpu.VMEM((HEADS, 16, N), BF16),
            pltpu.VMEM((HEADS, 16, N), BF16),
            pltpu.VMEM((HEADS, N + 8, N), F32),
            square(HEADS),
            square(HEADS, 2, 2),
            square(HEADS, 2),
            square(HEADS, 2),
            square(SIDE, 2),
            square(2),
            square(SIDE - 1, 2),
            square(SIDE - 1, 2),
            square(),
            square(SIDE),
            square(HEADS),
            square(2, HEADS),
            square(HEADS),
            square(HEADS),
            square(HEADS),
            square(HEADS),
            square(HEADS),
            square(HEADS),
            square(HEADS),
            pltpu.VMEM((HEADS, 8, N), F32),
            pltpu.VMEM((HEADS, 8, N), F32),
            pltpu.VMEM((HEADS, N + 8, N), F32),
            sem, sem,
            sem((HEADS,)), sem((HEADS,)),
            sem((HEADS,)), sem((SIDE,)),
            sem((SIDE, 2)), sem((SIDE, 2)),
            sem((SIDE,)), sem((HEADS,)),
            sem((HEADS,)), sem((HEADS,)),
            sem, sem,
        ],
        compiler_params=pltpu.CompilerParams(
            collective_id=0, has_side_effects=True, vmem_limit_bytes=40 * 2**20
        ),
        name="delta_backward",
    )(queries, keys, values_in, out_grad, logged_keep_factor, beta, conv_weight)


def solution(mesh):
    in_specs = (
        P("head", "ctx", None),
        P("head", "ctx", None),
        P("head", "ctx", None),
        P("head", "ctx", None),
        P("head", "ctx", None),
        P("head", "ctx"),
        P(None, "head", None),
    )
    out_specs = (P("head", "ctx", None), P("head", "ctx", None))
    return jax.shard_map(local, mesh=mesh, in_specs=in_specs, out_specs=out_specs, check_vma=False)
```

```python
import jax
import jax.numpy as jnp
from jax import lax
from jax.experimental import pallas as pl
from jax.experimental.pallas import tpu as pltpu
from jax.sharding import PartitionSpec as P

MESH = pl.DeviceIdType.MESH
F32 = jnp.float32
BF16 = jnp.bfloat16
HEADS = 4
N = 128
SIDE = 4
RING = 32


def split(a):
    high = a.astype(BF16)
    return high, (a - high.astype(F32)).astype(BF16)


def left(a):
    return jnp.concatenate(split(a), axis=1)


def right(*arrays):
    row = jnp.concatenate([part for a in arrays for part in split(a)], axis=1)
    return jnp.concatenate([row, row], axis=0)


def right_t(a):
    high, low = split(a)
    return jnp.concatenate(
        [jnp.concatenate([high, high], axis=1), jnp.concatenate([low, low], axis=1)], axis=0
    )


def halves(wide):
    return [
        wide[:, 2 * N * i : 2 * N * i + N] + wide[:, 2 * N * i + N : 2 * N * (i + 1)]
        for i in range(wide.shape[1] // (2 * N))
    ]


def mm(a, *bs):
    out = halves(jnp.dot(left(a), right(*bs), preferred_element_type=F32))
    return out[0] if len(bs) == 1 else out


def mm_t(a, b):
    return halves(
        lax.dot_general(
            left(a), right_t(b), (((1,), (1,)), ((), ())), preferred_element_type=F32
        )
    )[0]


def mm_exact(a, b):
    return jnp.dot(left(a), jnp.concatenate([b, b], axis=0), preferred_element_type=F32)


def kernel(
    q_hbm, k_hbm, v_hbm, o_hbm, g_hbm, beta_hbm, w_hbm, qg_ref, ig_ref,
    q_ref, k_ref, v_ref, o_ref, g_ref, beta_ref, w_ref,
    halo_v, padded, dsig, loc, pair, chip, row, tot, above, pref, start, sends, back, other,
    inv, rhs, ke, xv, xk, pl_mix, wt, lg, kgc, e0, e1, pg_first, pg_next, pg_pad,
    load_s,
    tail_s, tail_r, pair_s, pair_r, row_s, row_r, up_s, up_r, back_s, back_r, fwd_s, fwd_r, pg_s, pg_r,
):
    me = lax.axis_index("ctx")
    head = lax.axis_index("head")
    c = lax.rem(me, 2)
    x = lax.rem(me // 2, SIDE)
    y = me // (2 * SIDE)

    def at(yy, xx, cc):
        return ((yy * SIDE + xx) * 2 + cc, head)

    def place(v):
        return v * (2 * c - 1) + (SIDE - 1) * (1 - c)

    p, r = place(x), place(y)
    partner = at(y, x, 1 - c)
    following = (lax.rem(me + 1, RING), head)
    preceding = (lax.rem(me + RING - 1, RING), head)
    other_near = (lax.rem(me + 2 * c - 1 + RING, RING), head)

    loads = [
        pltpu.make_async_copy(src, dst, load_s.at[i])
        for i, (src, dst) in enumerate(
            (
                (k_hbm, k_ref), (g_hbm, g_ref), (beta_hbm, beta_ref), (q_hbm, q_ref),
                (o_hbm, o_ref), (v_hbm, v_ref), (w_hbm, w_ref),
            )
        )
    ]
    for load in loads:
        load.start()

    barrier = pltpu.get_barrier_semaphore()
    greeted = [partner, other_near]
    greeted += [at(y, lax.rem(x + d, SIDE), c) for d in range(1, SIDE)]
    greeted += [at(lax.rem(y + d, SIDE), x, c) for d in range(1, SIDE)]
    for device in greeted:
        pl.semaphore_signal(barrier, inc=1, device_id=device, device_id_type=MESH)

    def remote(src, dst, send, recv, device):
        return pltpu.make_async_remote_copy(
            src_ref=src, dst_ref=dst, send_sem=send, recv_sem=recv,
            device_id=device, device_id_type=MESH,
        )

    pending = []

    t_id = lax.broadcasted_iota(jnp.int32, (N, N), 0)
    s_id = lax.broadcasted_iota(jnp.int32, (N, N), 1)
    lower_ones = jnp.where(t_id >= s_id, 1.0, 0.0).astype(BF16)
    eye = jnp.where(t_id == s_id, 1.0, 0.0).astype(F32)

    def block_mask(small, large):
        return (t_id // large == s_id // large) & (t_id // small > s_id // small)

    heads = range(HEADS)
    system, kd_all, ket_all, kdt_all, qto_all, keep_all, beta_col_all, qn_all = [[] for _ in range(8)]
    for load in loads[:3]:
        load.wait()
    since_all, full_all = [], []
    for h in heads:
        k = k_ref[h].astype(F32)
        k = k * lax.rsqrt(jnp.sum(k * k, axis=1, keepdims=True) + 1e-6)
        g = g_ref[h]
        g_high = g.astype(BF16)
        rest = g - g_high.astype(F32)
        g_mid = rest.astype(BF16)
        g_low = (rest - g_mid.astype(F32)).astype(BF16)
        sums = jnp.dot(
            lower_ones, jnp.concatenate([g_high, g_mid, g_low], axis=1), preferred_element_type=F32
        )
        ld = sums[:, :N] + (sums[:, N : 2 * N] + sums[:, 2 * N :])
        middle = ld[N // 2 - 1 : N // 2, :]
        last = ld[N - 1 :, :]
        since = jnp.exp(ld - middle)
        until = jnp.exp(middle - ld)
        full = since * jnp.exp(middle)
        to_end = until * jnp.exp(last - middle)
        e1[h] = since
        e0[h] = full
        beta_row = beta_ref[h : h + 1, :]
        k_until = k * until
        kgc[h] = k_until
        mix = mm_t(k * since, k_until)
        system.append(jnp.where(t_id > s_id, mix * beta_row, 0.0))
        beta_col_all.append(jnp.sum(eye * beta_row, axis=1, keepdims=True))
        kd_all.append(k * full)
        qn_all.append(k * to_end)
        since_all.append(since)
        full_all.append(full)
        keep_all.append(jnp.exp(last))

    pl.semaphore_wait(barrier, len(greeted))
    tail_copy = remote(v_hbm.at[:, N - 16 :, :], halo_v, tail_s, tail_r, following)
    tail_copy.start()
    pending.append(tail_copy.wait_send)
    for load in loads[3:]:
        load.wait()

    inverse = [eye - jnp.where(block_mask(1, 2), system[h], 0.0) for h in heads]
    for small in (2, 8, 32):
        mask = block_mask(small, 4 * small)
        for h in heads:
            m = mm(inverse[h], jnp.where(mask, system[h], 0.0))
            squared, applied = mm(m, m, inverse[h])
            z = inverse[h] - applied
            inverse[h] = z + mm(squared, z)
    for h in heads:
        inv[h] = inverse[h]
        k_end = qn_all[h]
        ket_all.append(k_end.T * beta_ref[h : h + 1, :])
        ke[h] = k_end * beta_col_all[h]
        kdt_all.append(kd_all[h].T)
        q = q_ref[h].astype(F32)
        q = q * lax.rsqrt(jnp.sum(q * q, axis=1, keepdims=True) + 1e-6)
        upper = jnp.where(s_id >= t_id, mm_t(kgc[h], q * since_all[h]), 0.0)
        rhs[h] = beta_col_all[h] * mm_exact(upper, o_ref[h])
        qto_all.append(mm_exact((q * full_all[h]).T, o_ref[h]))

    tail_copy.wait_recv()
    pair_copies = []
    for h in heads:
        padded[h, 8:, :] = v_ref[h].astype(F32)
        edge = halo_v[h].astype(F32)[8:, :]
        padded[h, :8, :] = jnp.where(me > 0, edge, 0.0)
        pre = w_ref[0, h : h + 1, :] * padded[h, 8:, :]
        for j in range(1, 4):
            pre = pre + w_ref[j, h : h + 1, :] * padded[h, 8 - j : 8 - j + N, :]
        sig = jax.nn.sigmoid(pre)
        dsig[h] = sig * (1.0 + pre * (1.0 - sig))
        value = pre * sig
        keys_x, values_x = mm(inverse[h], kd_all[h], value)
        keys_xt = mm_t(kdt_all[h], inverse[h])
        fwd_t, fwd_f = mm(ket_all[h], keys_x, values_x)
        bwd_t, bwd_f = mm(keys_xt, ke[h], rhs[h])
        keep = eye * keep_all[h]
        loc[h, 0, 0] = keep - fwd_t
        loc[h, 0, 1] = fwd_f
        loc[h, 1, 0] = keep - bwd_t
        loc[h, 1, 1] = qto_all[h] - bwd_f
        xk[h] = keys_x
        xv[h] = values_x
        copy = remote(loc.at[h, c], pair.at[h], pair_s.at[h], pair_r.at[h], partner)
        copy.start()
        pair_copies.append(copy)
        pending.append(copy.wait_send)

    for d in (2, 1, 3, 0):
        h = lax.rem(x + d, SIDE)
        remote(loc.at[h, c], pair.at[h], pair_s.at[h], pair_r.at[h], partner).wait_recv()
        g_chip, f_chip = mm(loc[h, 1 - c, 0], pair[h, 0], pair[h, 1])
        if d == 0:
            row[p, 0] = g_chip
            row[p, 1] = f_chip + loc[h, 1 - c, 1]
        else:
            chip[d, 0] = g_chip
            chip[d, 1] = f_chip + loc[h, 1 - c, 1]
            copy = remote(chip.at[d], row.at[p], row_s.at[d], row_r.at[p], at(y, h, c))
            copy.start()
            pending.append(copy.wait_send)

    for h in heads:
        out_values = lax.dot_general(
            jnp.concatenate([o_ref[h], o_ref[h]], axis=1), jnp.concatenate(split(xv[h]), axis=1),
            (((1,), (1,)), ((), ())), preferred_element_type=F32,
        )
        pl_mix[h] = jnp.where(t_id >= s_id, out_values, 0.0) * beta_ref[h : h + 1, :]
        wt[h], lg[h] = mm(inv[h].T, ke[h], rhs[h])

    @pl.when(c == 0)
    def _():
        for h in heads:
            through, extra = mm(wt[h], pair[h, 0], pair[h, 1])
            wt[h] = through
            lg[h] = lg[h] + extra

    for d in range(1, SIDE):
        source = lax.rem(x + d, SIDE)
        slot = place(source)
        remote(chip.at[0], row.at[slot], row_s.at[0], row_r.at[slot], at(y, source, c)).wait_recv()
    p2, o2 = mm(row[1, 0], row[0, 0], row[0, 1])
    o2 = o2 + row[1, 1]
    q2, r2 = mm(row[3, 0], row[2, 0], row[2, 1])
    r2 = r2 + row[3, 1]
    tg, tf = mm(q2, p2, o2)
    tot[0] = tg
    tot[1] = tf + r2

    def up(kind, target):
        return remote(
            tot.at[kind], above.at[r, kind], up_s.at[target, kind], up_r.at[r, kind],
            at(place(target), x, c),
        )

    for target in range(1, SIDE):
        @pl.when(r < target)
        def _():
            up(1, target).start()

        @pl.when((r < target) & (r > 0))
        def _():
            up(0, target).start()

        def drain(target=target):
            @pl.when(r < target)
            def _():
                up(1, target).wait_send()

            @pl.when((r < target) & (r > 0))
            def _():
                up(0, target).wait_send()

        pending.append(drain)

    p3, o3 = mm(row[2, 0], p2, o2)
    pref[0, 0] = row[0, 0]
    pref[0, 1] = row[0, 1]
    pref[1, 0] = p2
    pref[1, 1] = o2
    pref[2, 0] = p3
    pref[2, 1] = o3 + row[2, 1]

    def got(source, kind):
        remote(
            tot.at[kind], above.at[source, kind], up_s.at[1, kind], up_r.at[source, kind], partner
        ).wait_recv()

    start[...] = jnp.zeros((N, N), F32)

    @pl.when(r >= 1)
    def _():
        got(0, 1)
        start[...] = above[0, 1]

    for source in (1, 2):
        @pl.when(r > source)
        def _():
            got(source, 0)
            got(source, 1)
            start[...] = mm(above[source, 0], start[...]) + above[source, 1]

    for target in range(SIDE):
        if target == 0:
            sends[0] = start[...]
        else:
            sends[target] = mm(pref[target - 1, 0], start[...]) + pref[target - 1, 1]
        to = place(target)
        copy = remote(
            sends.at[target], back.at[x], back_s.at[target], back_r.at[x], at(y, to, c)
        )

        @pl.when(to != x)
        def _():
            copy.start()

        @pl.when(to == x)
        def _():
            back[x] = sends[target]

        def drain(to=to, copy=copy):
            @pl.when(to != x)
            def _():
                copy.wait_send()

        pending.append(drain)

    forwards = [
        remote(back.at[h], other.at[h], fwd_s.at[h], fwd_r.at[h], partner) for h in heads
    ]

    def hand_on():
        for h in heads:
            @pl.when(x != h)
            def _():
                remote(sends.at[0], back.at[h], back_s.at[0], back_r.at[h], partner).wait_recv()

            forwards[h].start()

    def gradients(carries):
        for h in heads:
            if carries is other:
                forwards[h].wait_recv()
            pg = (lg[h] + mm(wt[h], carries[h])) * dsig[h]
            pg_pad[h, :N, :] = pg
            pg_first[h] = pg[:8, :]

    def queries(h, state):
        reach = lax.dot_general(
            jnp.concatenate([o_ref[h], o_ref[h]], axis=1),
            jnp.concatenate(split(state), axis=1),
            (((1,), (1,)), ((), ())), preferred_element_type=F32,
        )
        mixed = mm_t(reach, xk[h])
        weights = pl_mix[h] - jnp.where(t_id >= s_id, mixed, 0.0) * beta_ref[h : h + 1, :]
        qg_ref[h] = e1[h] * mm(weights, kgc[h]) + e0[h] * reach

    pg_copy = remote(pg_first, pg_next, pg_s, pg_r, preceding)

    @pl.when(c == 0)
    def _():
        hand_on()
        gradients(back)
        pg_copy.start()
        for h in heads:
            forwards[h].wait_recv()
            queries(h, other[h])

    @pl.when(c == 1)
    def _():
        hand_on()
        for h in heads:
            queries(h, mm(pair[h, 0], back[h]) + pair[h, 1])
        gradients(other)
        pg_copy.start()

    pending += [pg_copy.wait_send] + [copy.wait_send for copy in forwards]
    body = N - 8

    def mixed_rows(h, first, count):
        grad = w_ref[0, h : h + 1, :] * pg_pad[h, first : first + count, :]
        for j in range(1, 4):
            grad = grad + w_ref[j, h : h + 1, :] * pg_pad[h, first + j : first + j + count, :]
        ig_ref[h, first : first + count, :] = grad

    for h in heads:
        mixed_rows(h, 0, body)
    pg_copy.wait_recv()
    for h in heads:
        pg_pad[h, N:, :] = jnp.where(me < RING - 1, pg_next[h], 0.0)
        mixed_rows(h, body, 8)
    for wait in pending:
        wait()


def deliver(qg_from, ig_from, qg_to, ig_to, sems):
    copies = [
        pltpu.make_async_copy(src.at[h], dst.at[h], sems.at[i, h])
        for i, (src, dst) in enumerate(((qg_from, qg_to), (ig_from, ig_to)))
        for h in range(HEADS)
    ]
    for copy in copies:
        copy.start()
    for copy in copies:
        copy.wait()


def local(queries, keys, values_in, out_grad, logged_keep_factor, beta, conv_weight):
    vmem = pl.BlockSpec(memory_space=pltpu.VMEM)
    hbm = pl.BlockSpec(memory_space=pltpu.HBM)
    sem = pltpu.SemaphoreType.DMA
    square = lambda *lead: pltpu.VMEM((*lead, N, N), F32)
    out = jax.ShapeDtypeStruct((HEADS, N, N), F32)
    grads = pl.pallas_call(
        kernel,
        out_shape=(pltpu.VMEM((HEADS, N, N), F32),) * 2,
        in_specs=[hbm] * 7,
        out_specs=(vmem, vmem),
        scratch_shapes=[
            pltpu.VMEM((HEADS, N, N), BF16),
            pltpu.VMEM((HEADS, N, N), BF16),
            pltpu.VMEM((HEADS, N, N), BF16),
            pltpu.VMEM((HEADS, N, N), BF16),
            square(HEADS),
            pltpu.VMEM((HEADS, N), F32),
            pltpu.VMEM((4, HEADS, N), F32),
            pltpu.VMEM((HEADS, 16, N), BF16),
            pltpu.VMEM((HEADS, N + 8, N), F32),
            square(HEADS),
            square(HEADS, 2, 2),
            square(HEADS, 2),
            square(SIDE, 2),
            square(SIDE, 2),
            square(2),
            square(SIDE - 1, 2),
            square(SIDE - 1, 2),
            square(),
            square(SIDE),
            square(HEADS),
            square(HEADS),
            square(HEADS),
            square(HEADS),
            square(HEADS),
            square(HEADS),
            square(HEADS),
            square(HEADS),
            square(HEADS),
            square(HEADS),
            square(HEADS),
            square(HEADS),
            square(HEADS),
            pltpu.VMEM((HEADS, 8, N), F32),
            pltpu.VMEM((HEADS, 8, N), F32),
            pltpu.VMEM((HEADS, N + 8, N), F32),
            sem((7,)),
            sem, sem,
            sem((HEADS,)), sem((HEADS,)),
            sem((SIDE,)), sem((SIDE,)),
            sem((SIDE, 2)), sem((SIDE, 2)),
            sem((SIDE,)), sem((HEADS,)),
            sem((HEADS,)), sem((HEADS,)),
            sem, sem,
        ],
        compiler_params=pltpu.CompilerParams(
            collective_id=0, has_side_effects=True, vmem_limit_bytes=56 * 2**20
        ),
        name="delta_backward",
    )(queries, keys, values_in, out_grad, logged_keep_factor, beta, conv_weight)
    return pl.pallas_call(
        deliver,
        out_shape=(out, out),
        in_specs=[vmem] * 2,
        out_specs=(hbm, hbm),
        scratch_shapes=[sem((2, HEADS))],
        compiler_params=pltpu.CompilerParams(vmem_limit_bytes=8 * 2**20),
        name="deliver",
    )(*grads)


def solution(mesh):
    in_specs = (
        P("head", "ctx", None),
        P("head", "ctx", None),
        P("head", "ctx", None),
        P("head", "ctx", None),
        P("head", "ctx", None),
        P("head", "ctx"),
        P(None, "head", None),
    )
    out_specs = (P("head", "ctx", None), P("head", "ctx", None))
    return jax.shard_map(local, mesh=mesh, in_specs=in_specs, out_specs=out_specs, check_vma=False)
```

```python
import jax
import jax.numpy as jnp
from jax import lax
from jax.experimental import pallas as pl
from jax.experimental.pallas import tpu as pltpu
from jax.sharding import PartitionSpec as P

MESH = pl.DeviceIdType.MESH
F32 = jnp.float32
BF16 = jnp.bfloat16
HEADS = 4
N = 128
SIDE = 4
RING = 32


def split(a):
    high = a.astype(BF16)
    return high, (a - high.astype(F32)).astype(BF16)


def left(a):
    return jnp.concatenate(split(a), axis=1)


def right(*arrays):
    row = jnp.concatenate([part for a in arrays for part in split(a)], axis=1)
    return jnp.concatenate([row, row], axis=0)


def right_t(a):
    high, low = split(a)
    return jnp.concatenate(
        [jnp.concatenate([high, high], axis=1), jnp.concatenate([low, low], axis=1)], axis=0
    )


def halves(wide):
    return [
        wide[:, 2 * N * i : 2 * N * i + N] + wide[:, 2 * N * i + N : 2 * N * (i + 1)]
        for i in range(wide.shape[1] // (2 * N))
    ]


def mm(a, *bs):
    out = halves(jnp.dot(left(a), right(*bs), preferred_element_type=F32))
    return out[0] if len(bs) == 1 else out


def mm_t(a, b):
    return halves(
        lax.dot_general(
            left(a), right_t(b), (((1,), (1,)), ((), ())), preferred_element_type=F32
        )
    )[0]


def mm_exact(a, b):
    return jnp.dot(left(a), jnp.concatenate([b, b], axis=0), preferred_element_type=F32)


def kernel(
    q_hbm, k_hbm, v_hbm, o_hbm, g_hbm, beta_hbm, w_hbm, qg_ref, ig_ref,
    q_ref, k_ref, v_ref, o_ref, g_ref, beta_ref, w_ref,
    halo_v, padded, dsig, loc, pair, chip, row, tot, above, pref, start, sends, back, other,
    inv, rhs, ke, xv, xk, pl_mix, wt, lg, kgc, e0, e1, edge_out, edge_in, edge_pre, edges, near, pg_next, pg_pad,
    load_s,
    tail_s, tail_r, pair_s, pair_r, row_s, row_r, up_s, up_r, back_s, back_r, fwd_s, fwd_r, pg_s, pg_r, edge_s, edge_r,
    near_s, near_r,
):
    me = lax.axis_index("ctx")
    head = lax.axis_index("head")
    c = lax.rem(me, 2)
    x = lax.rem(me // 2, SIDE)
    y = me // (2 * SIDE)

    def at(yy, xx, cc):
        return ((yy * SIDE + xx) * 2 + cc, head)

    def place(v):
        return v * (2 * c - 1) + (SIDE - 1) * (1 - c)

    p, r = place(x), place(y)
    partner = at(y, x, 1 - c)
    following = (lax.rem(me + 1, RING), head)

    def before(chip_x):
        return lax.rem((y * SIDE + chip_x) * 2 + RING - 1, RING)

    next_row = lax.rem(me + 1, RING) // (2 * SIDE)
    other_near = (lax.rem(me + 2 * c - 1 + RING, RING), head)

    loads = [
        pltpu.make_async_copy(src, dst, load_s.at[i])
        for i, (src, dst) in enumerate(
            (
                (k_hbm, k_ref), (g_hbm, g_ref), (beta_hbm, beta_ref), (q_hbm, q_ref),
                (o_hbm, o_ref), (v_hbm, v_ref), (w_hbm, w_ref),
            )
        )
    ]
    for load in loads:
        load.start()

    barrier = pltpu.get_barrier_semaphore()
    greeted = [partner, other_near]
    greeted += [at(y, lax.rem(x + d, SIDE), c) for d in range(1, SIDE)]
    greeted += [at(lax.rem(y + d, SIDE), x, c) for d in range(1, SIDE)]
    greeted += [
        (jnp.where(c == 0, before(i), (next_row * SIDE + i) * 2), head) for i in range(SIDE)
    ]
    for device in greeted:
        pl.semaphore_signal(barrier, inc=1, device_id=device, device_id_type=MESH)

    def remote(src, dst, send, recv, device):
        return pltpu.make_async_remote_copy(
            src_ref=src, dst_ref=dst, send_sem=send, recv_sem=recv,
            device_id=device, device_id_type=MESH,
        )

    pending = []

    t_id = lax.broadcasted_iota(jnp.int32, (N, N), 0)
    s_id = lax.broadcasted_iota(jnp.int32, (N, N), 1)
    lower_ones = jnp.where(t_id >= s_id, 1.0, 0.0).astype(BF16)
    eye = jnp.where(t_id == s_id, 1.0, 0.0).astype(F32)

    def block_mask(small, large):
        return (t_id // large == s_id // large) & (t_id // small > s_id // small)

    heads = range(HEADS)
    system, kd_all, ket_all, kdt_all, qto_all, keep_all, beta_col_all, qn_all = [[] for _ in range(8)]
    for load in loads[:3]:
        load.wait()
    since_all, full_all = [], []
    for h in heads:
        k = k_ref[h].astype(F32)
        k = k * lax.rsqrt(jnp.sum(k * k, axis=1, keepdims=True) + 1e-6)
        g = g_ref[h]
        g_high = g.astype(BF16)
        rest = g - g_high.astype(F32)
        g_mid = rest.astype(BF16)
        g_low = (rest - g_mid.astype(F32)).astype(BF16)
        sums = jnp.dot(
            lower_ones, jnp.concatenate([g_high, g_mid, g_low], axis=1), preferred_element_type=F32
        )
        ld = sums[:, :N] + (sums[:, N : 2 * N] + sums[:, 2 * N :])
        middle = ld[N // 2 - 1 : N // 2, :]
        last = ld[N - 1 :, :]
        since = jnp.exp(ld - middle)
        until = jnp.exp(middle - ld)
        full = since * jnp.exp(middle)
        to_end = until * jnp.exp(last - middle)
        e1[h] = since
        e0[h] = full
        beta_row = beta_ref[h : h + 1, :]
        k_until = k * until
        kgc[h] = k_until
        mix = mm_t(k * since, k_until)
        system.append(jnp.where(t_id > s_id, mix * beta_row, 0.0))
        beta_col_all.append(jnp.sum(eye * beta_row, axis=1, keepdims=True))
        kd_all.append(k * full)
        qn_all.append(k * to_end)
        since_all.append(since)
        full_all.append(full)
        keep_all.append(jnp.exp(last))

    pl.semaphore_wait(barrier, len(greeted))
    tail_copy = remote(v_hbm.at[:, N - 16 :, :], halo_v, tail_s, tail_r, following)
    tail_copy.start()
    pending.append(tail_copy.wait_send)
    for load in loads[3:]:
        load.wait()

    inverse = [eye - jnp.where(block_mask(1, 2), system[h], 0.0) for h in heads]
    for small in (2, 8, 32):
        mask = block_mask(small, 4 * small)
        for h in heads:
            m = mm(inverse[h], jnp.where(mask, system[h], 0.0))
            squared, applied = mm(m, m, inverse[h])
            z = inverse[h] - applied
            inverse[h] = z + mm(squared, z)
    for h in heads:
        inv[h] = inverse[h]
        k_end = qn_all[h]
        ket_all.append(k_end.T * beta_ref[h : h + 1, :])
        ke[h] = k_end * beta_col_all[h]
        kdt_all.append(kd_all[h].T)
        q = q_ref[h].astype(F32)
        q = q * lax.rsqrt(jnp.sum(q * q, axis=1, keepdims=True) + 1e-6)
        upper = jnp.where(s_id >= t_id, mm_t(kgc[h], q * since_all[h]), 0.0)
        rhs[h] = beta_col_all[h] * mm_exact(upper, o_ref[h])
        qto_all.append(mm_exact((q * full_all[h]).T, o_ref[h]))

    tail_copy.wait_recv()
    pair_copies = []
    for h in heads:
        padded[h, 8:, :] = v_ref[h].astype(F32)
        edge = halo_v[h].astype(F32)[8:, :]
        padded[h, :8, :] = jnp.where(me > 0, edge, 0.0)
        pre = w_ref[0, h : h + 1, :] * padded[h, 8:, :]
        for j in range(1, 4):
            pre = pre + w_ref[j, h : h + 1, :] * padded[h, 8 - j : 8 - j + N, :]
        sig = jax.nn.sigmoid(pre)
        dsig[h] = sig * (1.0 + pre * (1.0 - sig))
        value = pre * sig
        keys_x, values_x = mm(inverse[h], kd_all[h], value)
        keys_xt = mm_t(kdt_all[h], inverse[h])
        fwd_t, fwd_f = mm(ket_all[h], keys_x, values_x)
        bwd_t, bwd_f = mm(keys_xt, ke[h], rhs[h])
        keep = eye * keep_all[h]
        loc[h, 0, 0] = keep - fwd_t
        loc[h, 0, 1] = fwd_f
        loc[h, 1, 0] = keep - bwd_t
        loc[h, 1, 1] = qto_all[h] - bwd_f
        xk[h] = keys_x
        xv[h] = values_x
        copy = remote(loc.at[h, c], pair.at[h], pair_s.at[h], pair_r.at[h], partner)
        copy.start()
        pair_copies.append(copy)
        pending.append(copy.wait_send)

    for d in (2, 1, 3, 0):
        h = lax.rem(x + d, SIDE)
        remote(loc.at[h, c], pair.at[h], pair_s.at[h], pair_r.at[h], partner).wait_recv()
        g_chip, f_chip = mm(loc[h, 1 - c, 0], pair[h, 0], pair[h, 1])
        if d == 0:
            row[p, 0] = g_chip
            row[p, 1] = f_chip + loc[h, 1 - c, 1]
        else:
            chip[d, 0] = g_chip
            chip[d, 1] = f_chip + loc[h, 1 - c, 1]
            copy = remote(chip.at[d], row.at[p], row_s.at[d], row_r.at[p], at(y, h, c))
            copy.start()
            pending.append(copy.wait_send)

    for h in heads:
        out_values = lax.dot_general(
            jnp.concatenate([o_ref[h], o_ref[h]], axis=1), jnp.concatenate(split(xv[h]), axis=1),
            (((1,), (1,)), ((), ())), preferred_element_type=F32,
        )
        pl_mix[h] = jnp.where(t_id >= s_id, out_values, 0.0) * beta_ref[h : h + 1, :]
        wt[h], lg[h] = mm(inv[h].T, ke[h], rhs[h])

    @pl.when(c == 0)
    def _():
        for h in heads:
            through, extra = mm(wt[h], pair[h, 0], pair[h, 1])
            wt[h] = through
            lg[h] = lg[h] + extra

    for h in heads:
        edge_out[h, 0] = wt[h, :8, :]
        edge_out[h, 1] = lg[h, :8, :]
        edge_out[h, 2] = dsig[h, :8, :]
    near_copy = remote(edge_out, near, near_s, near_r, partner)
    edge_copies = [
        remote(
            edge_out.at[lax.rem(x + d, SIDE)], edge_in.at[p], edge_s.at[d], edge_r.at[p],
            at(y, lax.rem(x + d, SIDE), c),
        )
        for d in range(1, SIDE)
    ]

    @pl.when(c == 1)
    def _():
        near_copy.start()

    @pl.when(c == 0)
    def _():
        for copy in edge_copies:
            copy.start()
        edge_in[p] = edge_out[x]

    for d in range(1, SIDE):
        source = lax.rem(x + d, SIDE)
        slot = place(source)
        remote(chip.at[0], row.at[slot], row_s.at[0], row_r.at[slot], at(y, source, c)).wait_recv()
    p2, o2 = mm(row[1, 0], row[0, 0], row[0, 1])
    o2 = o2 + row[1, 1]
    q2, r2 = mm(row[3, 0], row[2, 0], row[2, 1])
    r2 = r2 + row[3, 1]
    tg, tf = mm(q2, p2, o2)
    tot[0] = tg
    tot[1] = tf + r2

    def up(kind, target):
        return remote(
            tot.at[kind], above.at[r, kind], up_s.at[target, kind], up_r.at[r, kind],
            at(place(target), x, c),
        )

    for target in range(1, SIDE):
        @pl.when(r < target)
        def _():
            up(1, target).start()

        @pl.when((r < target) & (r > 0))
        def _():
            up(0, target).start()

        def drain(target=target):
            @pl.when(r < target)
            def _():
                up(1, target).wait_send()

            @pl.when((r < target) & (r > 0))
            def _():
                up(0, target).wait_send()

        pending.append(drain)

    p3, o3 = mm(row[2, 0], p2, o2)
    pref[0, 0] = row[0, 0]
    pref[0, 1] = row[0, 1]
    pref[1, 0] = p2
    pref[1, 1] = o2
    pref[2, 0] = p3
    pref[2, 1] = o3 + row[2, 1]

    @pl.when(c == 0)
    def _():
        for d in range(1, SIDE):
            slot = place(lax.rem(x + d, SIDE))
            remote(
                edge_out.at[0], edge_in.at[slot], edge_s.at[1], edge_r.at[slot], partner
            ).wait_recv()
        edge_pre[0, :8, :] = edge_in[0, 0]
        edge_pre[1, :8, :] = edge_in[0, 1]
        for i in range(1, SIDE):
            through, extra = mm(edge_in[i, 0], pref[i - 1, 0], pref[i - 1, 1])
            edge_pre[0, 8 * i : 8 * i + 8, :] = through
            edge_pre[1, 8 * i : 8 * i + 8, :] = extra + edge_in[i, 1]

    def got(source, kind):
        remote(
            tot.at[kind], above.at[source, kind], up_s.at[1, kind], up_r.at[source, kind], partner
        ).wait_recv()

    start[...] = jnp.zeros((N, N), F32)

    @pl.when(r >= 1)
    def _():
        got(0, 1)
        start[...] = above[0, 1]

    for source in (1, 2):
        @pl.when(r > source)
        def _():
            got(source, 0)
            got(source, 1)
            start[...] = mm(above[source, 0], start[...]) + above[source, 1]

    for target in range(SIDE):
        if target == 0:
            sends[0] = start[...]
        else:
            sends[target] = mm(pref[target - 1, 0], start[...]) + pref[target - 1, 1]
        to = place(target)
        copy = remote(
            sends.at[target], back.at[x], back_s.at[target], back_r.at[x], at(y, to, c)
        )

        @pl.when(to != x)
        def _():
            copy.start()

        @pl.when(to == x)
        def _():
            back[x] = sends[target]

        def drain(to=to, copy=copy):
            @pl.when(to != x)
            def _():
                copy.wait_send()

        pending.append(drain)

    edge_sends = [
        remote(edges.at[i], pg_next.at[x], pg_s.at[i], pg_r.at[x], (before(place(i)), head))
        for i in range(SIDE)
    ]

    @pl.when(c == 0)
    def _():
        first = edge_pre[1] + mm(edge_pre[0], start[...])
        for i in range(SIDE):
            edges[i] = first[8 * i : 8 * i + 8, :] * edge_in[i, 2]

            @pl.when((y > 0) | (place(i) > 0))
            def _():
                edge_sends[i].start()

    forwards = [
        remote(back.at[h], other.at[h], fwd_s.at[h], fwd_r.at[h], partner) for h in heads
    ]

    def hand_on():
        for h in heads:
            @pl.when(x != h)
            def _():
                remote(sends.at[0], back.at[h], back_s.at[0], back_r.at[h], partner).wait_recv()

            forwards[h].start()

    def queries(h, state):
        reach = lax.dot_general(
            jnp.concatenate([o_ref[h], o_ref[h]], axis=1),
            jnp.concatenate(split(state), axis=1),
            (((1,), (1,)), ((), ())), preferred_element_type=F32,
        )
        mixed = mm_t(reach, xk[h])
        weights = pl_mix[h] - jnp.where(t_id >= s_id, mixed, 0.0) * beta_ref[h : h + 1, :]
        qg_ref[h] = e1[h] * mm(weights, kgc[h]) + e0[h] * reach

    def take(own):
        @pl.when(own)
        def _():
            hand_on()

        @pl.when(jnp.logical_not(own))
        def _():
            for copy in forwards:
                copy.wait_recv()

    def query_side():
        take(c == 1)

        @pl.when(c == 1)
        def _():
            for h in heads:
                queries(h, mm(pair[h, 0], back[h]) + pair[h, 1])

        @pl.when(c == 0)
        def _():
            for h in heads:
                queries(h, other[h])

    def input_side():
        take(c == 0)

        @pl.when(c == 0)
        def _():
            near_copy.wait_recv()
            for h in heads:
                other_edge = near[h, 1] + mm(near[h, 0], back[h])
                pg_pad[h, N:, :] = other_edge * near[h, 2]
                pg_pad[h, :N, :] = (lg[h] + mm(wt[h], back[h])) * dsig[h]

        @pl.when(c == 1)
        def _():
            for h in heads:
                pg_pad[h, :N, :] = (lg[h] + mm(wt[h], other[h])) * dsig[h]

            @pl.when(me == RING - 1)
            def _():
                pg_pad[:, N:, :] = jnp.zeros((HEADS, 8, N), F32)

            @pl.when(me < RING - 1)
            def _():
                for h in heads:
                    remote(edges.at[0], pg_next.at[h], pg_s.at[0], pg_r.at[h], partner).wait_recv()
                    pg_pad[h, N:, :] = pg_next[h]

        for h in heads:
            grad = w_ref[0, h : h + 1, :] * pg_pad[h, :N, :]
            for j in range(1, 4):
                grad = grad + w_ref[j, h : h + 1, :] * pg_pad[h, j : j + N, :]
            ig_ref[h] = grad

    queries_first = (y == 0) | ((c == 1) & (y < SIDE - 1))

    @pl.when(queries_first)
    def _():
        query_side()
        input_side()

    @pl.when(jnp.logical_not(queries_first))
    def _():
        input_side()
        query_side()

    @pl.when(c == 0)
    def _():
        for copy in edge_copies:
            copy.wait_send()
        for i in range(SIDE):
            @pl.when((y > 0) | (place(i) > 0))
            def _():
                edge_sends[i].wait_send()

    @pl.when(c == 1)
    def _():
        near_copy.wait_send()

    for copy in forwards:
        copy.wait_send()
    for wait in pending:
        wait()


def deliver(qg_from, ig_from, qg_to, ig_to, sems):
    copies = [
        pltpu.make_async_copy(src.at[h], dst.at[h], sems.at[i, h])
        for i, (src, dst) in enumerate(((qg_from, qg_to), (ig_from, ig_to)))
        for h in range(HEADS)
    ]
    for copy in copies:
        copy.start()
    for copy in copies:
        copy.wait()


def local(queries, keys, values_in, out_grad, logged_keep_factor, beta, conv_weight):
    vmem = pl.BlockSpec(memory_space=pltpu.VMEM)
    hbm = pl.BlockSpec(memory_space=pltpu.HBM)
    sem = pltpu.SemaphoreType.DMA
    square = lambda *lead: pltpu.VMEM((*lead, N, N), F32)
    out = jax.ShapeDtypeStruct((HEADS, N, N), F32)
    grads = pl.pallas_call(
        kernel,
        out_shape=(pltpu.VMEM((HEADS, N, N), F32),) * 2,
        in_specs=[hbm] * 7,
        out_specs=(vmem, vmem),
        scratch_shapes=[
            pltpu.VMEM((HEADS, N, N), BF16),
            pltpu.VMEM((HEADS, N, N), BF16),
            pltpu.VMEM((HEADS, N, N), BF16),
            pltpu.VMEM((HEADS, N, N), BF16),
            square(HEADS),
            pltpu.VMEM((HEADS, N), F32),
            pltpu.VMEM((4, HEADS, N), F32),
            pltpu.VMEM((HEADS, 16, N), BF16),
            pltpu.VMEM((HEADS, N + 8, N), F32),
            square(HEADS),
            square(HEADS, 2, 2),
            square(HEADS, 2),
            square(SIDE, 2),
            square(SIDE, 2),
            square(2),
            square(SIDE - 1, 2),
            square(SIDE - 1, 2),
            square(),
            square(SIDE),
            square(HEADS),
            square(HEADS),
            square(HEADS),
            square(HEADS),
            square(HEADS),
            square(HEADS),
            square(HEADS),
            square(HEADS),
            square(HEADS),
            square(HEADS),
            square(HEADS),
            square(HEADS),
            square(HEADS),
            pltpu.VMEM((HEADS, 3, 8, N), F32),
            pltpu.VMEM((SIDE, 3, 8, N), F32),
            pltpu.VMEM((2, 8 * SIDE, N), F32),
            pltpu.VMEM((SIDE, 8, N), F32),
            pltpu.VMEM((HEADS, 3, 8, N), F32),
            pltpu.VMEM((HEADS, 8, N), F32),
            pltpu.VMEM((HEADS, N + 8, N), F32),
            sem((7,)),
            sem, sem,
            sem((HEADS,)), sem((HEADS,)),
            sem((SIDE,)), sem((SIDE,)),
            sem((SIDE, 2)), sem((SIDE, 2)),
            sem((SIDE,)), sem((HEADS,)),
            sem((HEADS,)), sem((HEADS,)),
            sem((SIDE,)), sem((HEADS,)),
            sem((SIDE,)), sem((SIDE,)),
            sem, sem,
        ],
        compiler_params=pltpu.CompilerParams(
            collective_id=0, has_side_effects=True, vmem_limit_bytes=56 * 2**20
        ),
        name="delta_backward",
    )(queries, keys, values_in, out_grad, logged_keep_factor, beta, conv_weight)
    return pl.pallas_call(
        deliver,
        out_shape=(out, out),
        in_specs=[vmem] * 2,
        out_specs=(hbm, hbm),
        scratch_shapes=[sem((2, HEADS))],
        compiler_params=pltpu.CompilerParams(vmem_limit_bytes=8 * 2**20),
        name="deliver",
    )(*grads)


def solution(mesh):
    in_specs = (
        P("head", "ctx", None),
        P("head", "ctx", None),
        P("head", "ctx", None),
        P("head", "ctx", None),
        P("head", "ctx", None),
        P("head", "ctx"),
        P(None, "head", None),
    )
    out_specs = (P("head", "ctx", None), P("head", "ctx", None))
    return jax.shard_map(local, mesh=mesh, in_specs=in_specs, out_specs=out_specs, check_vma=False)
```

```python
import jax
import jax.numpy as jnp
from jax import lax
from jax.experimental import pallas as pl
from jax.experimental.pallas import tpu as pltpu
from jax.sharding import PartitionSpec as P

MESH = pl.DeviceIdType.MESH
F32 = jnp.float32
BF16 = jnp.bfloat16
HEADS = 4
N = 128
SIDE = 4
RING = 32


def split(a):
    high = a.astype(BF16)
    return high, (a - high.astype(F32)).astype(BF16)


def left(a):
    return jnp.concatenate(split(a), axis=1)


def right(*arrays):
    row = jnp.concatenate([part for a in arrays for part in split(a)], axis=1)
    return jnp.concatenate([row, row], axis=0)


def right_t(a):
    high, low = split(a)
    return jnp.concatenate(
        [jnp.concatenate([high, high], axis=1), jnp.concatenate([low, low], axis=1)], axis=0
    )


def halves(wide):
    return [
        wide[:, 2 * N * i : 2 * N * i + N] + wide[:, 2 * N * i + N : 2 * N * (i + 1)]
        for i in range(wide.shape[1] // (2 * N))
    ]


def mm(a, *bs):
    out = halves(jnp.dot(left(a), right(*bs), preferred_element_type=F32))
    return out[0] if len(bs) == 1 else out


def mm_t(a, b):
    return halves(
        lax.dot_general(
            left(a), right_t(b), (((1,), (1,)), ((), ())), preferred_element_type=F32
        )
    )[0]


def mm_exact(a, b):
    return jnp.dot(left(a), jnp.concatenate([b, b], axis=0), preferred_element_type=F32)


def kernel(
    q_hbm, k_hbm, v_hbm, o_hbm, g_hbm, beta_hbm, w_hbm, qg_ref, ig_ref,
    q_ref, k_ref, v_ref, o_ref, g_ref, beta_ref, w_ref,
    halo_v, padded, dsig, loc, pair, chip, row, tot, above, pref, start, sends, back, other,
    inv, rhs, ke, xv, xk, pl_mix, wt, lg, kgc, e0, e1, edge_out, edge_in, edge_pre, edges, near, pg_next, pg_pad,
    load_s,
    tail_s, tail_r, pair_s, pair_r, row_s, row_r, up_s, up_r, back_s, back_r, fwd_s, fwd_r, pg_s, pg_r, edge_s, edge_r,
    near_s, near_r,
):
    me = lax.axis_index("ctx")
    head = lax.axis_index("head")
    c = lax.rem(me, 2)
    x = lax.rem(me // 2, SIDE)
    y = me // (2 * SIDE)

    def at(yy, xx, cc):
        return ((yy * SIDE + xx) * 2 + cc, head)

    def place(v):
        return v * (2 * c - 1) + (SIDE - 1) * (1 - c)

    p, r = place(x), place(y)
    partner = at(y, x, 1 - c)
    following = (lax.rem(me + 1, RING), head)

    def before(chip_x):
        return lax.rem((y * SIDE + chip_x) * 2 + RING - 1, RING)

    next_row = lax.rem(me + 1, RING) // (2 * SIDE)
    other_near = (lax.rem(me + 2 * c - 1 + RING, RING), head)

    loads = [
        pltpu.make_async_copy(src, dst, load_s.at[i])
        for i, (src, dst) in enumerate(
            (
                (k_hbm, k_ref), (g_hbm, g_ref), (beta_hbm, beta_ref), (q_hbm, q_ref),
                (o_hbm, o_ref), (v_hbm, v_ref), (w_hbm, w_ref),
            )
        )
    ]
    for load in loads:
        load.start()

    barrier = pltpu.get_barrier_semaphore()
    greeted = [partner, other_near]
    greeted += [at(y, lax.rem(x + d, SIDE), c) for d in range(1, SIDE)]
    greeted += [at(lax.rem(y + d, SIDE), x, c) for d in range(1, SIDE)]
    greeted += [
        (jnp.where(c == 0, before(i), (next_row * SIDE + i) * 2), head) for i in range(SIDE)
    ]
    for device in greeted:
        pl.semaphore_signal(barrier, inc=1, device_id=device, device_id_type=MESH)

    def remote(src, dst, send, recv, device):
        return pltpu.make_async_remote_copy(
            src_ref=src, dst_ref=dst, send_sem=send, recv_sem=recv,
            device_id=device, device_id_type=MESH,
        )

    pending = []

    t_id = lax.broadcasted_iota(jnp.int32, (N, N), 0)
    s_id = lax.broadcasted_iota(jnp.int32, (N, N), 1)
    lower_ones = jnp.where(t_id >= s_id, 1.0, 0.0).astype(BF16)
    eye = jnp.where(t_id == s_id, 1.0, 0.0).astype(F32)

    def block_mask(small, large):
        return (t_id // large == s_id // large) & (t_id // small > s_id // small)

    heads = range(HEADS)
    order = [lax.rem(x + d, SIDE) for d in (2, 1, 3, 0)]
    held = [{} for _ in order]
    for load in loads[:3]:
        load.wait()

    def prepare(i):
        h, mine = order[i], held[i]
        k = k_ref[h].astype(F32)
        k = k * lax.rsqrt(jnp.sum(k * k, axis=1, keepdims=True) + 1e-6)
        g = g_ref[h]
        g_high = g.astype(BF16)
        rest = g - g_high.astype(F32)
        g_mid = rest.astype(BF16)
        g_low = (rest - g_mid.astype(F32)).astype(BF16)
        sums = jnp.dot(
            lower_ones, jnp.concatenate([g_high, g_mid, g_low], axis=1), preferred_element_type=F32
        )
        ld = sums[:, :N] + (sums[:, N : 2 * N] + sums[:, 2 * N :])
        middle = ld[N // 2 - 1 : N // 2, :]
        last = ld[N - 1 :, :]
        since = jnp.exp(ld - middle)
        until = jnp.exp(middle - ld)
        full = since * jnp.exp(middle)
        to_end = until * jnp.exp(last - middle)
        e1[h] = since
        e0[h] = full
        beta_row = beta_ref[pl.ds(h, 1), :]
        k_until = k * until
        kgc[h] = k_until
        mix = mm_t(k * since, k_until)
        mine["system"] = jnp.where(t_id > s_id, mix * beta_row, 0.0)
        mine["beta"] = jnp.sum(eye * beta_row, axis=1, keepdims=True)
        mine["kd"] = k * full
        mine["k_end"] = k * to_end
        mine["keep"] = jnp.exp(last)

    def invert(group):
        inverse = {i: eye - jnp.where(block_mask(1, 2), held[i]["system"], 0.0) for i in group}
        for small in (2, 8, 32):
            mask = block_mask(small, 4 * small)
            for i in group:
                m = mm(inverse[i], jnp.where(mask, held[i]["system"], 0.0))
                squared, applied = mm(m, m, inverse[i])
                z = inverse[i] - applied
                inverse[i] = z + mm(squared, z)
        for i in group:
            h, mine = order[i], held[i]
            mine["inverse"] = inverse[i]
            inv[h] = inverse[i]
            mine["ket"] = mine["k_end"].T * beta_ref[pl.ds(h, 1), :]
            mine["ke"] = mine["k_end"] * mine["beta"]
            ke[h] = mine["ke"]
            mine["kdt"] = mine["kd"].T
            q = q_ref[h].astype(F32)
            q = q * lax.rsqrt(jnp.sum(q * q, axis=1, keepdims=True) + 1e-6)
            upper = jnp.where(s_id >= t_id, mm_t(kgc[h], q * e1[h]), 0.0)
            mine["rhs"] = mine["beta"] * mm_exact(upper, o_ref[h])
            rhs[h] = mine["rhs"]
            mine["qto"] = mm_exact((q * e0[h]).T, o_ref[h])

    pair_copies = []

    def finish(i):
        h, mine = order[i], held[i]
        padded[h, 8:, :] = v_ref[h].astype(F32)
        edge = halo_v[h].astype(F32)[8:, :]
        padded[h, :8, :] = jnp.where(me > 0, edge, 0.0)
        pre = w_ref[0, pl.ds(h, 1), :] * padded[h, 8:, :]
        for j in range(1, 4):
            pre = pre + w_ref[j, pl.ds(h, 1), :] * padded[h, 8 - j : 8 - j + N, :]
        sig = jax.nn.sigmoid(pre)
        dsig[h] = sig * (1.0 + pre * (1.0 - sig))
        value = pre * sig
        keys_x, values_x = mm(mine["inverse"], mine["kd"], value)
        keys_xt = mm_t(mine["kdt"], mine["inverse"])
        fwd_t, fwd_f = mm(mine["ket"], keys_x, values_x)
        bwd_t, bwd_f = mm(keys_xt, mine["ke"], mine["rhs"])
        keep = eye * mine["keep"]
        loc[h, 0, 0] = keep - fwd_t
        loc[h, 0, 1] = fwd_f
        loc[h, 1, 0] = keep - bwd_t
        loc[h, 1, 1] = mine["qto"] - bwd_f
        xk[h] = keys_x
        xv[h] = values_x
        copy = remote(loc.at[h, c], pair.at[h], pair_s.at[h], pair_r.at[h], partner)
        copy.start()
        pair_copies.append(copy)
        pending.append(copy.wait_send)

    def combine(i):
        h = order[i]
        pair_copies[i].wait_recv()
        g_chip, f_chip = mm(loc[h, 1 - c, 0], pair[h, 0], pair[h, 1])
        if i == SIDE - 1:
            row[p, 0] = g_chip
            row[p, 1] = f_chip + loc[h, 1 - c, 1]
        else:
            chip[i, 0] = g_chip
            chip[i, 1] = f_chip + loc[h, 1 - c, 1]
            copy = remote(chip.at[i], row.at[p], row_s.at[i], row_r.at[p], at(y, h, c))
            copy.start()
            pending.append(copy.wait_send)

    for i in range(HEADS):
        prepare(i)
    pl.semaphore_wait(barrier, len(greeted))
    tail_copy = remote(v_hbm.at[:, N - 16 :, :], halo_v, tail_s, tail_r, following)
    tail_copy.start()
    pending.append(tail_copy.wait_send)
    for load in loads[3:]:
        load.wait()
    invert(range(HEADS))
    tail_copy.wait_recv()
    for i in range(HEADS):
        finish(i)
    for i in range(HEADS):
        combine(i)

    for h in heads:
        out_values = lax.dot_general(
            jnp.concatenate([o_ref[h], o_ref[h]], axis=1), jnp.concatenate(split(xv[h]), axis=1),
            (((1,), (1,)), ((), ())), preferred_element_type=F32,
        )
        pl_mix[h] = jnp.where(t_id >= s_id, out_values, 0.0) * beta_ref[h : h + 1, :]
        wt[h], lg[h] = mm(inv[h].T, ke[h], rhs[h])

    @pl.when(c == 0)
    def _():
        for h in heads:
            through, extra = mm(wt[h], pair[h, 0], pair[h, 1])
            wt[h] = through
            lg[h] = lg[h] + extra

    for h in heads:
        edge_out[h, 0] = wt[h, :8, :]
        edge_out[h, 1] = lg[h, :8, :]
        edge_out[h, 2] = dsig[h, :8, :]
    near_copy = remote(edge_out, near, near_s, near_r, partner)
    edge_copies = [
        remote(
            edge_out.at[lax.rem(x + d, SIDE)], edge_in.at[p], edge_s.at[d], edge_r.at[p],
            at(y, lax.rem(x + d, SIDE), c),
        )
        for d in range(1, SIDE)
    ]

    @pl.when(c == 1)
    def _():
        near_copy.start()

    @pl.when(c == 0)
    def _():
        for copy in edge_copies:
            copy.start()
        edge_in[p] = edge_out[x]

    for d in range(1, SIDE):
        source = lax.rem(x + d, SIDE)
        slot = place(source)
        remote(chip.at[0], row.at[slot], row_s.at[0], row_r.at[slot], at(y, source, c)).wait_recv()
    p2, o2 = mm(row[1, 0], row[0, 0], row[0, 1])
    o2 = o2 + row[1, 1]
    q2, r2 = mm(row[3, 0], row[2, 0], row[2, 1])
    r2 = r2 + row[3, 1]
    tg, tf = mm(q2, p2, o2)
    tot[0] = tg
    tot[1] = tf + r2

    def up(kind, target):
        return remote(
            tot.at[kind], above.at[r, kind], up_s.at[target, kind], up_r.at[r, kind],
            at(place(target), x, c),
        )

    for target in reversed(range(1, SIDE)):
        @pl.when(r < target)
        def _():
            up(1, target).start()

        @pl.when((r < target) & (r > 0))
        def _():
            up(0, target).start()

        def drain(target=target):
            @pl.when(r < target)
            def _():
                up(1, target).wait_send()

            @pl.when((r < target) & (r > 0))
            def _():
                up(0, target).wait_send()

        pending.append(drain)

    p3, o3 = mm(row[2, 0], p2, o2)
    pref[0, 0] = row[0, 0]
    pref[0, 1] = row[0, 1]
    pref[1, 0] = p2
    pref[1, 1] = o2
    pref[2, 0] = p3
    pref[2, 1] = o3 + row[2, 1]

    @pl.when(c == 0)
    def _():
        for d in range(1, SIDE):
            slot = place(lax.rem(x + d, SIDE))
            remote(
                edge_out.at[0], edge_in.at[slot], edge_s.at[1], edge_r.at[slot], partner
            ).wait_recv()
        edge_pre[0, :8, :] = edge_in[0, 0]
        edge_pre[1, :8, :] = edge_in[0, 1]
        for i in range(1, SIDE):
            through, extra = mm(edge_in[i, 0], pref[i - 1, 0], pref[i - 1, 1])
            edge_pre[0, 8 * i : 8 * i + 8, :] = through
            edge_pre[1, 8 * i : 8 * i + 8, :] = extra + edge_in[i, 1]

    def got(source, kind):
        remote(
            tot.at[kind], above.at[source, kind], up_s.at[1, kind], up_r.at[source, kind], partner
        ).wait_recv()

    start[...] = jnp.zeros((N, N), F32)

    @pl.when(r >= 1)
    def _():
        got(0, 1)
        start[...] = above[0, 1]

    for source in (1, 2):
        @pl.when(r > source)
        def _():
            got(source, 0)
            got(source, 1)
            start[...] = mm(above[source, 0], start[...]) + above[source, 1]

    for target in range(SIDE):
        if target == 0:
            sends[0] = start[...]
        else:
            sends[target] = mm(pref[target - 1, 0], start[...]) + pref[target - 1, 1]
        to = place(target)
        copy = remote(
            sends.at[target], back.at[x], back_s.at[target], back_r.at[x], at(y, to, c)
        )

        @pl.when(to != x)
        def _():
            copy.start()

        @pl.when(to == x)
        def _():
            back[x] = sends[target]

        def drain(to=to, copy=copy):
            @pl.when(to != x)
            def _():
                copy.wait_send()

        pending.append(drain)

    edge_sends = [
        remote(edges.at[i], pg_next.at[x], pg_s.at[i], pg_r.at[x], (before(place(i)), head))
        for i in range(SIDE)
    ]

    @pl.when(c == 0)
    def _():
        first = edge_pre[1] + mm(edge_pre[0], start[...])
        for i in range(SIDE):
            edges[i] = first[8 * i : 8 * i + 8, :] * edge_in[i, 2]

            @pl.when((y > 0) | (place(i) > 0))
            def _():
                edge_sends[i].start()

    forwards = [
        remote(back.at[h], other.at[h], fwd_s.at[h], fwd_r.at[h], partner) for h in heads
    ]

    def hand_on():
        for h in heads:
            @pl.when(x != h)
            def _():
                remote(sends.at[0], back.at[h], back_s.at[0], back_r.at[h], partner).wait_recv()

            forwards[h].start()

    def queries(h, state):
        reach = lax.dot_general(
            jnp.concatenate([o_ref[h], o_ref[h]], axis=1),
            jnp.concatenate(split(state), axis=1),
            (((1,), (1,)), ((), ())), preferred_element_type=F32,
        )
        mixed = mm_t(reach, xk[h])
        weights = pl_mix[h] - jnp.where(t_id >= s_id, mixed, 0.0) * beta_ref[h : h + 1, :]
        qg_ref[h] = e1[h] * mm(weights, kgc[h]) + e0[h] * reach

    def take(own):
        @pl.when(own)
        def _():
            hand_on()

        @pl.when(jnp.logical_not(own))
        def _():
            for copy in forwards:
                copy.wait_recv()

    def query_side():
        take(c == 1)

        @pl.when(c == 1)
        def _():
            for h in heads:
                queries(h, mm(pair[h, 0], back[h]) + pair[h, 1])

        @pl.when(c == 0)
        def _():
            for h in heads:
                queries(h, other[h])

    def input_side():
        take(c == 0)

        @pl.when(c == 0)
        def _():
            near_copy.wait_recv()
            for h in heads:
                other_edge = near[h, 1] + mm(near[h, 0], back[h])
                pg_pad[h, N:, :] = other_edge * near[h, 2]
                pg_pad[h, :N, :] = (lg[h] + mm(wt[h], back[h])) * dsig[h]

        @pl.when(c == 1)
        def _():
            for h in heads:
                pg_pad[h, :N, :] = (lg[h] + mm(wt[h], other[h])) * dsig[h]

            @pl.when(me == RING - 1)
            def _():
                pg_pad[:, N:, :] = jnp.zeros((HEADS, 8, N), F32)

            @pl.when(me < RING - 1)
            def _():
                for h in heads:
                    remote(edges.at[0], pg_next.at[h], pg_s.at[0], pg_r.at[h], partner).wait_recv()
                    pg_pad[h, N:, :] = pg_next[h]

        for h in heads:
            grad = w_ref[0, h : h + 1, :] * pg_pad[h, :N, :]
            for j in range(1, 4):
                grad = grad + w_ref[j, h : h + 1, :] * pg_pad[h, j : j + N, :]
            ig_ref[h] = grad

    queries_first = (y == 0) | ((c == 1) & (y < SIDE - 1))

    @pl.when(queries_first)
    def _():
        query_side()
        input_side()

    @pl.when(jnp.logical_not(queries_first))
    def _():
        input_side()
        query_side()

    @pl.when(c == 0)
    def _():
        for copy in edge_copies:
            copy.wait_send()
        for i in range(SIDE):
            @pl.when((y > 0) | (place(i) > 0))
            def _():
                edge_sends[i].wait_send()

    @pl.when(c == 1)
    def _():
        near_copy.wait_send()

    for copy in forwards:
        copy.wait_send()
    for wait in pending:
        wait()


def deliver(qg_from, ig_from, qg_to, ig_to, sems):
    copies = [
        pltpu.make_async_copy(src.at[h], dst.at[h], sems.at[i, h])
        for i, (src, dst) in enumerate(((qg_from, qg_to), (ig_from, ig_to)))
        for h in range(HEADS)
    ]
    for copy in copies:
        copy.start()
    for copy in copies:
        copy.wait()


def local(queries, keys, values_in, out_grad, logged_keep_factor, beta, conv_weight):
    vmem = pl.BlockSpec(memory_space=pltpu.VMEM)
    hbm = pl.BlockSpec(memory_space=pltpu.HBM)
    sem = pltpu.SemaphoreType.DMA
    square = lambda *lead: pltpu.VMEM((*lead, N, N), F32)
    out = jax.ShapeDtypeStruct((HEADS, N, N), F32)
    grads = pl.pallas_call(
        kernel,
        out_shape=(pltpu.VMEM((HEADS, N, N), F32),) * 2,
        in_specs=[hbm] * 7,
        out_specs=(vmem, vmem),
        scratch_shapes=[
            pltpu.VMEM((HEADS, N, N), BF16),
            pltpu.VMEM((HEADS, N, N), BF16),
            pltpu.VMEM((HEADS, N, N), BF16),
            pltpu.VMEM((HEADS, N, N), BF16),
            square(HEADS),
            pltpu.VMEM((HEADS, N), F32),
            pltpu.VMEM((4, HEADS, N), F32),
            pltpu.VMEM((HEADS, 16, N), BF16),
            pltpu.VMEM((HEADS, N + 8, N), F32),
            square(HEADS),
            square(HEADS, 2, 2),
            square(HEADS, 2),
            square(SIDE, 2),
            square(SIDE, 2),
            square(2),
            square(SIDE - 1, 2),
            square(SIDE - 1, 2),
            square(),
            square(SIDE),
            square(HEADS),
            square(HEADS),
            square(HEADS),
            square(HEADS),
            square(HEADS),
            square(HEADS),
            square(HEADS),
            square(HEADS),
            square(HEADS),
            square(HEADS),
            square(HEADS),
            square(HEADS),
            square(HEADS),
            pltpu.VMEM((HEADS, 3, 8, N), F32),
            pltpu.VMEM((SIDE, 3, 8, N), F32),
            pltpu.VMEM((2, 8 * SIDE, N), F32),
            pltpu.VMEM((SIDE, 8, N), F32),
            pltpu.VMEM((HEADS, 3, 8, N), F32),
            pltpu.VMEM((HEADS, 8, N), F32),
            pltpu.VMEM((HEADS, N + 8, N), F32),
            sem((7,)),
            sem, sem,
            sem((HEADS,)), sem((HEADS,)),
            sem((SIDE,)), sem((SIDE,)),
            sem((SIDE, 2)), sem((SIDE, 2)),
            sem((SIDE,)), sem((HEADS,)),
            sem((HEADS,)), sem((HEADS,)),
            sem((SIDE,)), sem((HEADS,)),
            sem((SIDE,)), sem((SIDE,)),
            sem, sem,
        ],
        compiler_params=pltpu.CompilerParams(
            collective_id=0, has_side_effects=True, vmem_limit_bytes=56 * 2**20
        ),
        name="delta_backward",
    )(queries, keys, values_in, out_grad, logged_keep_factor, beta, conv_weight)
    return pl.pallas_call(
        deliver,
        out_shape=(out, out),
        in_specs=[vmem] * 2,
        out_specs=(hbm, hbm),
        scratch_shapes=[sem((2, HEADS))],
        compiler_params=pltpu.CompilerParams(vmem_limit_bytes=8 * 2**20),
        name="deliver",
    )(*grads)


def solution(mesh):
    in_specs = (
        P("head", "ctx", None),
        P("head", "ctx", None),
        P("head", "ctx", None),
        P("head", "ctx", None),
        P("head", "ctx", None),
        P("head", "ctx"),
        P(None, "head", None),
    )
    out_specs = (P("head", "ctx", None), P("head", "ctx", None))
    return jax.shard_map(local, mesh=mesh, in_specs=in_specs, out_specs=out_specs, check_vma=False)
```

```python
import jax
import jax.numpy as jnp
from jax import lax
from jax.experimental import pallas as pl
from jax.experimental.pallas import tpu as pltpu
from jax.sharding import PartitionSpec as P

MESH = pl.DeviceIdType.MESH
F32 = jnp.float32
BF16 = jnp.bfloat16
HEADS = 4
N = 128
SIDE = 4
RING = 32


def split(a):
    high = a.astype(BF16)
    return high, (a - high.astype(F32)).astype(BF16)


def left(a):
    return jnp.concatenate(split(a), axis=1)


def right(*arrays):
    row = jnp.concatenate([part for a in arrays for part in split(a)], axis=1)
    return jnp.concatenate([row, row], axis=0)


def right_t(a):
    high, low = split(a)
    return jnp.concatenate(
        [jnp.concatenate([high, high], axis=1), jnp.concatenate([low, low], axis=1)], axis=0
    )


def halves(wide):
    return [
        wide[:, 2 * N * i : 2 * N * i + N] + wide[:, 2 * N * i + N : 2 * N * (i + 1)]
        for i in range(wide.shape[1] // (2 * N))
    ]


def mm(a, *bs):
    out = halves(jnp.dot(left(a), right(*bs), preferred_element_type=F32))
    return out[0] if len(bs) == 1 else out


def mm_t(a, b):
    return halves(
        lax.dot_general(
            left(a), right_t(b), (((1,), (1,)), ((), ())), preferred_element_type=F32
        )
    )[0]


def mm_exact(a, b):
    return jnp.dot(left(a), jnp.concatenate([b, b], axis=0), preferred_element_type=F32)


def kernel(
    q_hbm, k_hbm, v_hbm, o_hbm, g_hbm, beta_hbm, w_hbm, qg_ref, ig_ref,
    q_ref, k_ref, v_ref, o_ref, g_ref, beta_ref, w_ref,
    halo_v, padded, dsig, loc, pair, chip, row, tot, above, pref, start, sends, back, other,
    inv, rhs, ke, xv, xk, pl_mix, wt, lg, kgc, e0, e1, edge_out, edge_in, edge_pre, edges, near, pg_next, pg_pad,
    load_s,
    tail_s, tail_r, pair_s, pair_r, row_s, row_r, up_s, up_r, back_s, back_r, fwd_s, fwd_r, pg_s, pg_r, edge_s, edge_r,
    near_s, near_r,
):
    me = lax.axis_index("ctx")
    head = lax.axis_index("head")
    c = lax.rem(me, 2)
    x = lax.rem(me // 2, SIDE)
    y = me // (2 * SIDE)

    def at(yy, xx, cc):
        return ((yy * SIDE + xx) * 2 + cc, head)

    def place(v):
        return v * (2 * c - 1) + (SIDE - 1) * (1 - c)

    p, r = place(x), place(y)
    partner = at(y, x, 1 - c)
    following = (lax.rem(me + 1, RING), head)

    def before(chip_x):
        return lax.rem((y * SIDE + chip_x) * 2 + RING - 1, RING)

    next_row = lax.rem(me + 1, RING) // (2 * SIDE)
    other_near = (lax.rem(me + 2 * c - 1 + RING, RING), head)

    loads = [
        pltpu.make_async_copy(src, dst, load_s.at[i])
        for i, (src, dst) in enumerate(
            (
                (k_hbm, k_ref), (g_hbm, g_ref), (beta_hbm, beta_ref), (q_hbm, q_ref),
                (o_hbm, o_ref), (v_hbm, v_ref), (w_hbm, w_ref),
            )
        )
    ]
    for load in loads:
        load.start()

    barrier = pltpu.get_barrier_semaphore()
    greeted = [partner, other_near]
    greeted += [at(y, lax.rem(x + d, SIDE), c) for d in range(1, SIDE)]
    greeted += [at(lax.rem(y + d, SIDE), x, c) for d in range(1, SIDE)]
    greeted += [
        (jnp.where(c == 0, before(i), (next_row * SIDE + i) * 2), head) for i in range(SIDE)
    ]
    for device in greeted:
        pl.semaphore_signal(barrier, inc=1, device_id=device, device_id_type=MESH)

    def remote(src, dst, send, recv, device):
        return pltpu.make_async_remote_copy(
            src_ref=src, dst_ref=dst, send_sem=send, recv_sem=recv,
            device_id=device, device_id_type=MESH,
        )

    pending = []

    t_id = lax.broadcasted_iota(jnp.int32, (N, N), 0)
    s_id = lax.broadcasted_iota(jnp.int32, (N, N), 1)
    lower_ones = jnp.where(t_id >= s_id, 1.0, 0.0).astype(BF16)
    eye = jnp.where(t_id == s_id, 1.0, 0.0).astype(F32)

    def block_mask(small, large):
        return (t_id // large == s_id // large) & (t_id // small > s_id // small)

    heads = range(HEADS)
    order = [lax.rem(x + d, SIDE) for d in (2, 1, 3, 0)]
    held = [{} for _ in order]
    for load in loads[:3]:
        load.wait()

    def prepare(i):
        h, mine = order[i], held[i]
        k = k_ref[h].astype(F32)
        k = k * lax.rsqrt(jnp.sum(k * k, axis=1, keepdims=True) + 1e-6)
        g = g_ref[h]
        g_high = g.astype(BF16)
        rest = g - g_high.astype(F32)
        g_mid = rest.astype(BF16)
        g_low = (rest - g_mid.astype(F32)).astype(BF16)
        sums = jnp.dot(
            lower_ones, jnp.concatenate([g_high, g_mid, g_low], axis=1), preferred_element_type=F32
        )
        ld = sums[:, :N] + (sums[:, N : 2 * N] + sums[:, 2 * N :])
        middle = ld[N // 2 - 1 : N // 2, :]
        last = ld[N - 1 :, :]
        since = jnp.exp(ld - middle)
        until = jnp.exp(middle - ld)
        full = since * jnp.exp(middle)
        to_end = until * jnp.exp(last - middle)
        e1[h] = since
        e0[h] = full
        beta_row = beta_ref[pl.ds(h, 1), :]
        k_until = k * until
        kgc[h] = k_until
        mix = mm_t(k * since, k_until)
        mine["system"] = jnp.where(t_id > s_id, mix * beta_row, 0.0)
        mine["beta"] = jnp.sum(eye * beta_row, axis=1, keepdims=True)
        mine["kd"] = k * full
        mine["k_end"] = k * to_end
        mine["keep"] = jnp.exp(last)

    def invert(group):
        inverse = {i: eye - jnp.where(block_mask(1, 2), held[i]["system"], 0.0) for i in group}
        for small in (2, 8, 32):
            mask = block_mask(small, 4 * small)
            for i in group:
                m = mm(inverse[i], jnp.where(mask, held[i]["system"], 0.0))
                squared, applied = mm(m, m, inverse[i])
                z = inverse[i] - applied
                inverse[i] = z + mm(squared, z)
        for i in group:
            h, mine = order[i], held[i]
            mine["inverse"] = inverse[i]
            inv[h] = inverse[i]
            mine["ket"] = mine["k_end"].T * beta_ref[pl.ds(h, 1), :]
            mine["ke"] = mine["k_end"] * mine["beta"]
            ke[h] = mine["ke"]
            mine["kdt"] = mine["kd"].T
            q = q_ref[h].astype(F32)
            q = q * lax.rsqrt(jnp.sum(q * q, axis=1, keepdims=True) + 1e-6)
            upper = jnp.where(s_id >= t_id, mm_t(kgc[h], q * e1[h]), 0.0)
            mine["rhs"] = mine["beta"] * mm_exact(upper, o_ref[h])
            rhs[h] = mine["rhs"]
            mine["qto"] = mm_exact((q * e0[h]).T, o_ref[h])

    pair_copies = []

    def finish(i):
        h, mine = order[i], held[i]
        padded[h, 8:, :] = v_ref[h].astype(F32)
        edge = halo_v[h].astype(F32)[8:, :]
        padded[h, :8, :] = jnp.where(me > 0, edge, 0.0)
        pre = w_ref[0, pl.ds(h, 1), :] * padded[h, 8:, :]
        for j in range(1, 4):
            pre = pre + w_ref[j, pl.ds(h, 1), :] * padded[h, 8 - j : 8 - j + N, :]
        sig = jax.nn.sigmoid(pre)
        dsig[h] = sig * (1.0 + pre * (1.0 - sig))
        value = pre * sig
        keys_x, values_x = mm(mine["inverse"], mine["kd"], value)
        keys_xt = mm_t(mine["kdt"], mine["inverse"])
        fwd_t, fwd_f = mm(mine["ket"], keys_x, values_x)
        bwd_t, bwd_f = mm(keys_xt, mine["ke"], mine["rhs"])
        keep = eye * mine["keep"]
        loc[h, 0, 0] = keep - fwd_t
        loc[h, 0, 1] = fwd_f
        loc[h, 1, 0] = keep - bwd_t
        loc[h, 1, 1] = mine["qto"] - bwd_f
        xk[h] = keys_x
        xv[h] = values_x
        copy = remote(loc.at[h, c], pair.at[h], pair_s.at[h], pair_r.at[h], partner)
        copy.start()
        pair_copies.append(copy)
        pending.append(copy.wait_send)

    def combine(i):
        h = order[i]
        pair_copies[i].wait_recv()
        g_chip, f_chip = mm(loc[h, 1 - c, 0], pair[h, 0], pair[h, 1])
        if i == SIDE - 1:
            row[p, 0] = g_chip
            row[p, 1] = f_chip + loc[h, 1 - c, 1]
        else:
            chip[i, 0] = g_chip
            chip[i, 1] = f_chip + loc[h, 1 - c, 1]
            copy = remote(chip.at[i], row.at[p], row_s.at[i], row_r.at[p], at(y, h, c))
            copy.start()
            pending.append(copy.wait_send)

    for i in range(HEADS):
        prepare(i)
    pl.semaphore_wait(barrier, len(greeted))
    tail_copy = remote(v_hbm.at[:, N - 16 :, :], halo_v, tail_s, tail_r, following)
    tail_copy.start()
    pending.append(tail_copy.wait_send)
    for load in loads[3:]:
        load.wait()
    invert(range(HEADS))
    tail_copy.wait_recv()
    for i in range(HEADS):
        finish(i)
    for i in range(HEADS):
        combine(i)

    for h in heads:
        out_values = lax.dot_general(
            jnp.concatenate([o_ref[h], o_ref[h]], axis=1), jnp.concatenate(split(xv[h]), axis=1),
            (((1,), (1,)), ((), ())), preferred_element_type=F32,
        )
        pl_mix[h] = jnp.where(t_id >= s_id, out_values, 0.0) * beta_ref[h : h + 1, :]
        wt[h], lg[h] = mm(inv[h].T, ke[h], rhs[h])

    @pl.when(c == 0)
    def _():
        for h in heads:
            through, extra = mm(wt[h], pair[h, 0], pair[h, 1])
            wt[h] = through
            lg[h] = lg[h] + extra

    for h in heads:
        edge_out[h, 0] = wt[h, :8, :]
        edge_out[h, 1] = lg[h, :8, :]
        edge_out[h, 2] = dsig[h, :8, :]
    near_copy = remote(edge_out, near, near_s, near_r, partner)
    edge_copies = [
        remote(
            edge_out.at[lax.rem(x + d, SIDE)], edge_in.at[p], edge_s.at[d], edge_r.at[p],
            at(y, lax.rem(x + d, SIDE), c),
        )
        for d in range(1, SIDE)
    ]

    @pl.when(c == 1)
    def _():
        near_copy.start()

    @pl.when(c == 0)
    def _():
        for copy in edge_copies:
            copy.start()
        edge_in[p] = edge_out[x]

    for d in range(1, SIDE):
        source = lax.rem(x + d, SIDE)
        slot = place(source)
        remote(chip.at[0], row.at[slot], row_s.at[0], row_r.at[slot], at(y, source, c)).wait_recv()
    p2, o2 = mm(row[1, 0], row[0, 0], row[0, 1])
    o2 = o2 + row[1, 1]
    q2, r2 = mm(row[3, 0], row[2, 0], row[2, 1])
    r2 = r2 + row[3, 1]
    tg, tf = mm(q2, p2, o2)
    tot[0] = tg
    tot[1] = tf + r2

    def up(kind, target):
        return remote(
            tot.at[kind], above.at[r, kind], up_s.at[target, kind], up_r.at[r, kind],
            at(place(target), x, c),
        )

    for target in reversed(range(1, SIDE)):
        @pl.when(r < target)
        def _():
            up(1, target).start()

        @pl.when((r < target) & (r > 0))
        def _():
            up(0, target).start()

        def drain(target=target):
            @pl.when(r < target)
            def _():
                up(1, target).wait_send()

            @pl.when((r < target) & (r > 0))
            def _():
                up(0, target).wait_send()

        pending.append(drain)

    p3, o3 = mm(row[2, 0], p2, o2)
    pref[0] = row[0]
    pref[1] = row[0]
    pref[2, 0] = p2
    pref[2, 1] = o2
    pref[3, 0] = p3
    pref[3, 1] = o3 + row[2, 1]

    @pl.when(c == 0)
    def _():
        for d in range(1, SIDE):
            slot = place(lax.rem(x + d, SIDE))
            remote(
                edge_out.at[0], edge_in.at[slot], edge_s.at[1], edge_r.at[slot], partner
            ).wait_recv()
        edge_pre[0, :8, :] = edge_in[0, 0]
        edge_pre[1, :8, :] = edge_in[0, 1]
        for i in range(1, SIDE):
            through, extra = mm(edge_in[i, 0], pref[i, 0], pref[i, 1])
            edge_pre[0, 8 * i : 8 * i + 8, :] = through
            edge_pre[1, 8 * i : 8 * i + 8, :] = extra + edge_in[i, 1]

    def got(source, kind):
        remote(
            tot.at[kind], above.at[source, kind], up_s.at[1, kind], up_r.at[source, kind], partner
        ).wait_recv()

    start[...] = jnp.zeros((N, N), F32)

    @pl.when(r >= 1)
    def _():
        got(0, 1)
        start[...] = above[0, 1]

    for source in (1, 2):
        @pl.when(r > source)
        def _():
            got(source, 0)
            got(source, 1)
            start[...] = mm(above[source, 0], start[...]) + above[source, 1]

    state = start[...]
    for d in (2, 1, 3, 0):
        to = lax.rem(x + d, SIDE)
        slot = place(to)
        later = mm(pref[slot, 0], state) + pref[slot, 1]
        there = jnp.where(slot == 0, state, later)
        if d == 0:
            back[x] = there
        else:
            sends[d] = there
            copy = remote(sends.at[d], back.at[x], back_s.at[d], back_r.at[x], at(y, to, c))
            copy.start()
            pending.append(copy.wait_send)

    edge_sends = [
        remote(edges.at[i], pg_next.at[x], pg_s.at[i], pg_r.at[x], (before(place(i)), head))
        for i in range(SIDE)
    ]

    @pl.when(c == 0)
    def _():
        first = edge_pre[1] + mm(edge_pre[0], start[...])
        for i in range(SIDE):
            edges[i] = first[8 * i : 8 * i + 8, :] * edge_in[i, 2]

            @pl.when((y > 0) | (place(i) > 0))
            def _():
                edge_sends[i].start()

    forwards = [
        remote(back.at[h], other.at[h], fwd_s.at[h], fwd_r.at[h], partner) for h in heads
    ]

    def hand_on():
        for d in (0, 1, 3, 2):
            h = lax.rem(x + d, SIDE)
            if d > 0:
                remote(sends.at[0], back.at[h], back_s.at[0], back_r.at[h], partner).wait_recv()
            remote(back.at[h], other.at[h], fwd_s.at[h], fwd_r.at[h], partner).start()

    def queries(h, state):
        reach = lax.dot_general(
            jnp.concatenate([o_ref[h], o_ref[h]], axis=1),
            jnp.concatenate(split(state), axis=1),
            (((1,), (1,)), ((), ())), preferred_element_type=F32,
        )
        mixed = mm_t(reach, xk[h])
        weights = pl_mix[h] - jnp.where(t_id >= s_id, mixed, 0.0) * beta_ref[h : h + 1, :]
        qg_ref[h] = e1[h] * mm(weights, kgc[h]) + e0[h] * reach

    def take(own):
        @pl.when(own)
        def _():
            hand_on()

        @pl.when(jnp.logical_not(own))
        def _():
            for copy in forwards:
                copy.wait_recv()

    def query_side():
        take(c == 1)

        @pl.when(c == 1)
        def _():
            for h in heads:
                queries(h, mm(pair[h, 0], back[h]) + pair[h, 1])

        @pl.when(c == 0)
        def _():
            for h in heads:
                queries(h, other[h])

    def input_side():
        take(c == 0)

        @pl.when(c == 0)
        def _():
            near_copy.wait_recv()
            for h in heads:
                other_edge = near[h, 1] + mm(near[h, 0], back[h])
                pg_pad[h, N:, :] = other_edge * near[h, 2]
                pg_pad[h, :N, :] = (lg[h] + mm(wt[h], back[h])) * dsig[h]

        @pl.when(c == 1)
        def _():
            for h in heads:
                pg_pad[h, :N, :] = (lg[h] + mm(wt[h], other[h])) * dsig[h]

            @pl.when(me == RING - 1)
            def _():
                pg_pad[:, N:, :] = jnp.zeros((HEADS, 8, N), F32)

            @pl.when(me < RING - 1)
            def _():
                for h in heads:
                    remote(edges.at[0], pg_next.at[h], pg_s.at[0], pg_r.at[h], partner).wait_recv()
                    pg_pad[h, N:, :] = pg_next[h]

        for h in heads:
            grad = w_ref[0, h : h + 1, :] * pg_pad[h, :N, :]
            for j in range(1, 4):
                grad = grad + w_ref[j, h : h + 1, :] * pg_pad[h, j : j + N, :]
            ig_ref[h] = grad

    queries_first = (y == 0) | ((c == 1) & (y < SIDE - 1))

    @pl.when(queries_first)
    def _():
        query_side()
        input_side()

    @pl.when(jnp.logical_not(queries_first))
    def _():
        input_side()
        query_side()

    @pl.when(c == 0)
    def _():
        for copy in edge_copies:
            copy.wait_send()
        for i in range(SIDE):
            @pl.when((y > 0) | (place(i) > 0))
            def _():
                edge_sends[i].wait_send()

    @pl.when(c == 1)
    def _():
        near_copy.wait_send()

    for copy in forwards:
        copy.wait_send()
    for wait in pending:
        wait()


def deliver(qg_from, ig_from, qg_to, ig_to, sems):
    copies = [
        pltpu.make_async_copy(src.at[h], dst.at[h], sems.at[i, h])
        for i, (src, dst) in enumerate(((qg_from, qg_to), (ig_from, ig_to)))
        for h in range(HEADS)
    ]
    for copy in copies:
        copy.start()
    for copy in copies:
        copy.wait()


def local(queries, keys, values_in, out_grad, logged_keep_factor, beta, conv_weight):
    vmem = pl.BlockSpec(memory_space=pltpu.VMEM)
    hbm = pl.BlockSpec(memory_space=pltpu.HBM)
    sem = pltpu.SemaphoreType.DMA
    square = lambda *lead: pltpu.VMEM((*lead, N, N), F32)
    out = jax.ShapeDtypeStruct((HEADS, N, N), F32)
    grads = pl.pallas_call(
        kernel,
        out_shape=(pltpu.VMEM((HEADS, N, N), F32),) * 2,
        in_specs=[hbm] * 7,
        out_specs=(vmem, vmem),
        scratch_shapes=[
            pltpu.VMEM((HEADS, N, N), BF16),
            pltpu.VMEM((HEADS, N, N), BF16),
            pltpu.VMEM((HEADS, N, N), BF16),
            pltpu.VMEM((HEADS, N, N), BF16),
            square(HEADS),
            pltpu.VMEM((HEADS, N), F32),
            pltpu.VMEM((4, HEADS, N), F32),
            pltpu.VMEM((HEADS, 16, N), BF16),
            pltpu.VMEM((HEADS, N + 8, N), F32),
            square(HEADS),
            square(HEADS, 2, 2),
            square(HEADS, 2),
            square(SIDE, 2),
            square(SIDE, 2),
            square(2),
            square(SIDE - 1, 2),
            square(SIDE, 2),
            square(),
            square(SIDE),
            square(HEADS),
            square(HEADS),
            square(HEADS),
            square(HEADS),
            square(HEADS),
            square(HEADS),
            square(HEADS),
            square(HEADS),
            square(HEADS),
            square(HEADS),
            square(HEADS),
            square(HEADS),
            square(HEADS),
            pltpu.VMEM((HEADS, 3, 8, N), F32),
            pltpu.VMEM((SIDE, 3, 8, N), F32),
            pltpu.VMEM((2, 8 * SIDE, N), F32),
            pltpu.VMEM((SIDE, 8, N), F32),
            pltpu.VMEM((HEADS, 3, 8, N), F32),
            pltpu.VMEM((HEADS, 8, N), F32),
            pltpu.VMEM((HEADS, N + 8, N), F32),
            sem((7,)),
            sem, sem,
            sem((HEADS,)), sem((HEADS,)),
            sem((SIDE,)), sem((SIDE,)),
            sem((SIDE, 2)), sem((SIDE, 2)),
            sem((SIDE,)), sem((HEADS,)),
            sem((HEADS,)), sem((HEADS,)),
            sem((SIDE,)), sem((HEADS,)),
            sem((SIDE,)), sem((SIDE,)),
            sem, sem,
        ],
        compiler_params=pltpu.CompilerParams(
            collective_id=0, has_side_effects=True, vmem_limit_bytes=56 * 2**20
        ),
        name="delta_backward",
    )(queries, keys, values_in, out_grad, logged_keep_factor, beta, conv_weight)
    return pl.pallas_call(
        deliver,
        out_shape=(out, out),
        in_specs=[vmem] * 2,
        out_specs=(hbm, hbm),
        scratch_shapes=[sem((2, HEADS))],
        compiler_params=pltpu.CompilerParams(vmem_limit_bytes=8 * 2**20),
        name="deliver",
    )(*grads)


def solution(mesh):
    in_specs = (
        P("head", "ctx", None),
        P("head", "ctx", None),
        P("head", "ctx", None),
        P("head", "ctx", None),
        P("head", "ctx", None),
        P("head", "ctx"),
        P(None, "head", None),
    )
    out_specs = (P("head", "ctx", None), P("head", "ctx", None))
    return jax.shard_map(local, mesh=mesh, in_specs=in_specs, out_specs=out_specs, check_vma=False)
```

```python
import jax
import jax.numpy as jnp
from jax import lax
from jax.experimental import pallas as pl
from jax.experimental.pallas import tpu as pltpu
from jax.sharding import PartitionSpec as P

MESH = pl.DeviceIdType.MESH
F32 = jnp.float32
BF16 = jnp.bfloat16
HEADS = 4
N = 128
SIDE = 4
RING = 32


def split(a):
    high = a.astype(BF16)
    return high, (a - high.astype(F32)).astype(BF16)


def left(a):
    return jnp.concatenate(split(a), axis=1)


def right(*arrays):
    row = jnp.concatenate([part for a in arrays for part in split(a)], axis=1)
    return jnp.concatenate([row, row], axis=0)


def right_t(a):
    high, low = split(a)
    return jnp.concatenate(
        [jnp.concatenate([high, high], axis=1), jnp.concatenate([low, low], axis=1)], axis=0
    )


def halves(wide):
    return [
        wide[:, 2 * N * i : 2 * N * i + N] + wide[:, 2 * N * i + N : 2 * N * (i + 1)]
        for i in range(wide.shape[1] // (2 * N))
    ]


def mm(a, *bs):
    out = halves(jnp.dot(left(a), right(*bs), preferred_element_type=F32))
    return out[0] if len(bs) == 1 else out


def mm_t(a, b):
    return halves(
        lax.dot_general(
            left(a), right_t(b), (((1,), (1,)), ((), ())), preferred_element_type=F32
        )
    )[0]


def mm_exact(a, b):
    return jnp.dot(left(a), jnp.concatenate([b, b], axis=0), preferred_element_type=F32)


def kernel(
    q_hbm, k_hbm, v_hbm, o_hbm, g_hbm, beta_hbm, w_hbm, qg_ref, ig_ref,
    q_ref, k_ref, v_ref, o_ref, g_ref, beta_ref, w_ref,
    halo_v, padded, dsig, loc, pair, chip, row, tot, above, pref, start, sends, back, other,
    inv, rhs, ke, xv, xk, pl_mix, wt, lg, kgc, e0, e1, edge_out, edge_in, edge_pre, edges, near, pg_next, pg_pad,
    load_s,
    tail_s, tail_r, pair_s, pair_r, row_s, row_r, up_s, up_r, back_s, back_r, fwd_s, fwd_r, pg_s, pg_r, edge_s, edge_r,
    near_s, near_r,
):
    me = lax.axis_index("ctx")
    head = lax.axis_index("head")
    c = lax.rem(me, 2)
    x = lax.rem(me // 2, SIDE)
    y = me // (2 * SIDE)

    def at(yy, xx, cc):
        return ((yy * SIDE + xx) * 2 + cc, head)

    def place(v):
        return v * (2 * c - 1) + (SIDE - 1) * (1 - c)

    p, r = place(x), place(y)
    partner = at(y, x, 1 - c)
    following = (lax.rem(me + 1, RING), head)

    def before(chip_x):
        return lax.rem((y * SIDE + chip_x) * 2 + RING - 1, RING)

    next_row = lax.rem(me + 1, RING) // (2 * SIDE)
    other_near = (lax.rem(me + 2 * c - 1 + RING, RING), head)

    loads = [
        pltpu.make_async_copy(src, dst, load_s.at[i])
        for i, (src, dst) in enumerate(
            (
                (k_hbm, k_ref), (g_hbm, g_ref), (beta_hbm, beta_ref), (q_hbm, q_ref),
                (o_hbm, o_ref), (v_hbm, v_ref), (w_hbm, w_ref),
            )
        )
    ]
    for load in loads:
        load.start()

    barrier = pltpu.get_barrier_semaphore()
    greeted = [partner, other_near]
    greeted += [at(y, lax.rem(x + d, SIDE), c) for d in range(1, SIDE)]
    greeted += [at(lax.rem(y + d, SIDE), x, c) for d in range(1, SIDE)]
    greeted += [
        (jnp.where(c == 0, before(i), (next_row * SIDE + i) * 2), head) for i in range(SIDE)
    ]
    for device in greeted:
        pl.semaphore_signal(barrier, inc=1, device_id=device, device_id_type=MESH)

    def remote(src, dst, send, recv, device):
        return pltpu.make_async_remote_copy(
            src_ref=src, dst_ref=dst, send_sem=send, recv_sem=recv,
            device_id=device, device_id_type=MESH,
        )

    pending = []

    t_id = lax.broadcasted_iota(jnp.int32, (N, N), 0)
    s_id = lax.broadcasted_iota(jnp.int32, (N, N), 1)
    lower_ones = jnp.where(t_id >= s_id, 1.0, 0.0).astype(BF16)
    eye = jnp.where(t_id == s_id, 1.0, 0.0).astype(F32)

    def block_mask(small, large):
        return (t_id // large == s_id // large) & (t_id // small > s_id // small)

    heads = range(HEADS)
    order = [lax.rem(x + d, SIDE) for d in (2, 1, 3, 0)]
    held = [{} for _ in order]
    for load in loads[:3]:
        load.wait()

    def prepare(i):
        h, mine = order[i], held[i]
        k = k_ref[h].astype(F32)
        k = k * lax.rsqrt(jnp.sum(k * k, axis=1, keepdims=True) + 1e-6)
        g = g_ref[h]
        g_high = g.astype(BF16)
        rest = g - g_high.astype(F32)
        g_mid = rest.astype(BF16)
        g_low = (rest - g_mid.astype(F32)).astype(BF16)
        sums = jnp.dot(
            lower_ones, jnp.concatenate([g_high, g_mid, g_low], axis=1), preferred_element_type=F32
        )
        ld = sums[:, :N] + (sums[:, N : 2 * N] + sums[:, 2 * N :])
        middle = ld[N // 2 - 1 : N // 2, :]
        last = ld[N - 1 :, :]
        since = jnp.exp(ld - middle)
        until = jnp.exp(middle - ld)
        full = since * jnp.exp(middle)
        to_end = until * jnp.exp(last - middle)
        e1[h] = since
        e0[h] = full
        beta_row = beta_ref[pl.ds(h, 1), :]
        k_until = k * until
        kgc[h] = k_until
        mix = mm_t(k * since, k_until)
        mine["system"] = jnp.where(t_id > s_id, mix * beta_row, 0.0)
        mine["beta"] = jnp.sum(eye * beta_row, axis=1, keepdims=True)
        mine["kd"] = k * full
        mine["k_end"] = k * to_end
        mine["keep"] = jnp.exp(last)

    def invert(group):
        inverse = {i: eye - jnp.where(block_mask(1, 2), held[i]["system"], 0.0) for i in group}
        for small in (2, 8, 32):
            mask = block_mask(small, 4 * small)
            for i in group:
                m = mm(inverse[i], jnp.where(mask, held[i]["system"], 0.0))
                squared, applied = mm(m, m, inverse[i])
                z = inverse[i] - applied
                inverse[i] = z + mm(squared, z)
        for i in group:
            h, mine = order[i], held[i]
            mine["inverse"] = inverse[i]
            inv[h] = inverse[i]
            mine["ket"] = mine["k_end"].T * beta_ref[pl.ds(h, 1), :]
            mine["ke"] = mine["k_end"] * mine["beta"]
            ke[h] = mine["ke"]
            mine["kdt"] = mine["kd"].T
            q = q_ref[h].astype(F32)
            q = q * lax.rsqrt(jnp.sum(q * q, axis=1, keepdims=True) + 1e-6)
            upper = jnp.where(s_id >= t_id, mm_t(kgc[h], q * e1[h]), 0.0)
            mine["rhs"] = mine["beta"] * mm_exact(upper, o_ref[h])
            rhs[h] = mine["rhs"]
            mine["qto"] = mm_exact((q * e0[h]).T, o_ref[h])

    pair_copies = []

    def finish(i):
        h, mine = order[i], held[i]
        padded[h, 8:, :] = v_ref[h].astype(F32)
        edge = halo_v[h].astype(F32)[8:, :]
        padded[h, :8, :] = jnp.where(me > 0, edge, 0.0)
        pre = w_ref[0, pl.ds(h, 1), :] * padded[h, 8:, :]
        for j in range(1, 4):
            pre = pre + w_ref[j, pl.ds(h, 1), :] * padded[h, 8 - j : 8 - j + N, :]
        sig = jax.nn.sigmoid(pre)
        dsig[h] = sig * (1.0 + pre * (1.0 - sig))
        value = pre * sig
        keys_x, values_x = mm(mine["inverse"], mine["kd"], value)
        keys_xt = mm_t(mine["kdt"], mine["inverse"])
        fwd_t, fwd_f = mm(mine["ket"], keys_x, values_x)
        bwd_t, bwd_f = mm(keys_xt, mine["ke"], mine["rhs"])
        keep = eye * mine["keep"]
        loc[h, 0, 0] = keep - fwd_t
        loc[h, 0, 1] = fwd_f
        loc[h, 1, 0] = keep - bwd_t
        loc[h, 1, 1] = mine["qto"] - bwd_f
        xk[h] = keys_x
        xv[h] = values_x
        copy = remote(loc.at[h, c], pair.at[h], pair_s.at[h], pair_r.at[h], partner)
        copy.start()
        pair_copies.append(copy)
        pending.append(copy.wait_send)

    def combine(i):
        h = order[i]
        pair_copies[i].wait_recv()
        g_chip, f_chip = mm(loc[h, 1 - c, 0], pair[h, 0], pair[h, 1])
        if i == SIDE - 1:
            row[p, 0] = g_chip
            row[p, 1] = f_chip + loc[h, 1 - c, 1]
        else:
            chip[i, 0] = g_chip
            chip[i, 1] = f_chip + loc[h, 1 - c, 1]
            copy = remote(chip.at[i], row.at[p], row_s.at[i], row_r.at[p], at(y, h, c))
            copy.start()
            pending.append(copy.wait_send)

    for i in range(HEADS):
        prepare(i)
    pl.semaphore_wait(barrier, len(greeted))
    tail_copy = remote(v_hbm.at[:, N - 16 :, :], halo_v, tail_s, tail_r, following)
    tail_copy.start()
    pending.append(tail_copy.wait_send)
    for load in loads[3:]:
        load.wait()
    invert(range(HEADS))
    tail_copy.wait_recv()
    for i in range(HEADS):
        finish(i)
    for i in range(HEADS):
        combine(i)

    for h in heads:
        out_values = lax.dot_general(
            jnp.concatenate([o_ref[h], o_ref[h]], axis=1), jnp.concatenate(split(xv[h]), axis=1),
            (((1,), (1,)), ((), ())), preferred_element_type=F32,
        )
        pl_mix[h] = jnp.where(t_id >= s_id, out_values, 0.0) * beta_ref[h : h + 1, :]
        wt[h], lg[h] = mm(inv[h].T, ke[h], rhs[h])

    @pl.when(c == 0)
    def _():
        for h in heads:
            through, extra = mm(wt[h], pair[h, 0], pair[h, 1])
            wt[h] = through
            lg[h] = lg[h] + extra

    for h in heads:
        edge_out[h, 0] = wt[h, :8, :]
        edge_out[h, 1] = lg[h, :8, :]
        edge_out[h, 2] = dsig[h, :8, :]
    near_copy = remote(edge_out, near, near_s, near_r, partner)
    edge_copies = [
        remote(
            edge_out.at[lax.rem(x + d, SIDE)], edge_in.at[p], edge_s.at[d], edge_r.at[p],
            at(y, lax.rem(x + d, SIDE), c),
        )
        for d in range(1, SIDE)
    ]

    @pl.when(c == 1)
    def _():
        near_copy.start()

    @pl.when(c == 0)
    def _():
        for copy in edge_copies:
            copy.start()
        edge_in[p] = edge_out[x]

    for d in range(1, SIDE):
        source = lax.rem(x + d, SIDE)
        slot = place(source)
        remote(chip.at[0], row.at[slot], row_s.at[0], row_r.at[slot], at(y, source, c)).wait_recv()
    p2, o2 = mm(row[1, 0], row[0, 0], row[0, 1])
    o2 = o2 + row[1, 1]
    q2, r2 = mm(row[3, 0], row[2, 0], row[2, 1])
    r2 = r2 + row[3, 1]
    tot[1] = mm(q2, o2) + r2

    def up(kind, target):
        return remote(
            tot.at[kind], above.at[r, kind], up_s.at[target, kind], up_r.at[r, kind],
            at(place(target), x, c),
        )

    for target in reversed(range(1, SIDE)):
        @pl.when(r < target)
        def _():
            up(1, target).start()

    tot[0] = mm(q2, p2)
    for target in reversed(range(1, SIDE)):
        @pl.when((r < target) & (r > 0))
        def _():
            up(0, target).start()

        def drain(target=target):
            @pl.when(r < target)
            def _():
                up(1, target).wait_send()

            @pl.when((r < target) & (r > 0))
            def _():
                up(0, target).wait_send()

        pending.append(drain)

    p3, o3 = mm(row[2, 0], p2, o2)
    pref[0] = row[0]
    pref[1] = row[0]
    pref[2, 0] = p2
    pref[2, 1] = o2
    pref[3, 0] = p3
    pref[3, 1] = o3 + row[2, 1]

    @pl.when(c == 0)
    def _():
        for d in range(1, SIDE):
            slot = place(lax.rem(x + d, SIDE))
            remote(
                edge_out.at[0], edge_in.at[slot], edge_s.at[1], edge_r.at[slot], partner
            ).wait_recv()
        edge_pre[0, :8, :] = edge_in[0, 0]
        edge_pre[1, :8, :] = edge_in[0, 1]
        for i in range(1, SIDE):
            through, extra = mm(edge_in[i, 0], pref[i, 0], pref[i, 1])
            edge_pre[0, 8 * i : 8 * i + 8, :] = through
            edge_pre[1, 8 * i : 8 * i + 8, :] = extra + edge_in[i, 1]

    def got(source, kind):
        remote(
            tot.at[kind], above.at[source, kind], up_s.at[1, kind], up_r.at[source, kind], partner
        ).wait_recv()

    start[...] = jnp.zeros((N, N), F32)

    @pl.when(r >= 1)
    def _():
        got(0, 1)
        start[...] = above[0, 1]

    for source in (1, 2):
        @pl.when(r > source)
        def _():
            got(source, 0)
            got(source, 1)
            start[...] = mm(above[source, 0], start[...]) + above[source, 1]

    state = start[...]
    for d in (2, 1, 3, 0):
        to = lax.rem(x + d, SIDE)
        slot = place(to)
        later = mm(pref[slot, 0], state) + pref[slot, 1]
        there = jnp.where(slot == 0, state, later)
        if d == 0:
            back[x] = there
        else:
            sends[d] = there
            copy = remote(sends.at[d], back.at[x], back_s.at[d], back_r.at[x], at(y, to, c))
            copy.start()
            pending.append(copy.wait_send)

    edge_sends = [
        remote(edges.at[i], pg_next.at[x], pg_s.at[i], pg_r.at[x], (before(place(i)), head))
        for i in range(SIDE)
    ]

    @pl.when(c == 0)
    def _():
        first = edge_pre[1] + mm(edge_pre[0], start[...])
        for i in range(SIDE):
            edges[i] = first[8 * i : 8 * i + 8, :] * edge_in[i, 2]

            @pl.when((y > 0) | (place(i) > 0))
            def _():
                edge_sends[i].start()

    forwards = [
        remote(back.at[h], other.at[h], fwd_s.at[h], fwd_r.at[h], partner) for h in heads
    ]

    def hand_on():
        for d in (0, 1, 3, 2):
            h = lax.rem(x + d, SIDE)
            if d > 0:
                remote(sends.at[0], back.at[h], back_s.at[0], back_r.at[h], partner).wait_recv()
            remote(back.at[h], other.at[h], fwd_s.at[h], fwd_r.at[h], partner).start()

    def queries(h, state):
        reach = lax.dot_general(
            jnp.concatenate([o_ref[h], o_ref[h]], axis=1),
            jnp.concatenate(split(state), axis=1),
            (((1,), (1,)), ((), ())), preferred_element_type=F32,
        )
        mixed = mm_t(reach, xk[h])
        weights = pl_mix[h] - jnp.where(t_id >= s_id, mixed, 0.0) * beta_ref[h : h + 1, :]
        qg_ref[h] = e1[h] * mm(weights, kgc[h]) + e0[h] * reach

    def take(own):
        @pl.when(own)
        def _():
            hand_on()

        @pl.when(jnp.logical_not(own))
        def _():
            for copy in forwards:
                copy.wait_recv()

    def query_side():
        take(c == 1)

        @pl.when(c == 1)
        def _():
            for h in heads:
                queries(h, mm(pair[h, 0], back[h]) + pair[h, 1])

        @pl.when(c == 0)
        def _():
            for h in heads:
                queries(h, other[h])

    def input_side():
        take(c == 0)

        @pl.when(c == 0)
        def _():
            near_copy.wait_recv()
            for h in heads:
                other_edge = near[h, 1] + mm(near[h, 0], back[h])
                pg_pad[h, N:, :] = other_edge * near[h, 2]
                pg_pad[h, :N, :] = (lg[h] + mm(wt[h], back[h])) * dsig[h]

        @pl.when(c == 1)
        def _():
            for h in heads:
                pg_pad[h, :N, :] = (lg[h] + mm(wt[h], other[h])) * dsig[h]

            @pl.when(me == RING - 1)
            def _():
                pg_pad[:, N:, :] = jnp.zeros((HEADS, 8, N), F32)

            @pl.when(me < RING - 1)
            def _():
                for h in heads:
                    remote(edges.at[0], pg_next.at[h], pg_s.at[0], pg_r.at[h], partner).wait_recv()
                    pg_pad[h, N:, :] = pg_next[h]

        for h in heads:
            grad = w_ref[0, h : h + 1, :] * pg_pad[h, :N, :]
            for j in range(1, 4):
                grad = grad + w_ref[j, h : h + 1, :] * pg_pad[h, j : j + N, :]
            ig_ref[h] = grad

    queries_first = (y == 0) | ((c == 1) & (y < SIDE - 1))

    @pl.when(queries_first)
    def _():
        query_side()
        input_side()

    @pl.when(jnp.logical_not(queries_first))
    def _():
        input_side()
        query_side()

    @pl.when(c == 0)
    def _():
        for copy in edge_copies:
            copy.wait_send()
        for i in range(SIDE):
            @pl.when((y > 0) | (place(i) > 0))
            def _():
                edge_sends[i].wait_send()

    @pl.when(c == 1)
    def _():
        near_copy.wait_send()

    for copy in forwards:
        copy.wait_send()
    for wait in pending:
        wait()


def deliver(qg_from, ig_from, qg_to, ig_to, sems):
    copies = [
        pltpu.make_async_copy(src.at[h], dst.at[h], sems.at[i, h])
        for i, (src, dst) in enumerate(((qg_from, qg_to), (ig_from, ig_to)))
        for h in range(HEADS)
    ]
    for copy in copies:
        copy.start()
    for copy in copies:
        copy.wait()


def local(queries, keys, values_in, out_grad, logged_keep_factor, beta, conv_weight):
    vmem = pl.BlockSpec(memory_space=pltpu.VMEM)
    hbm = pl.BlockSpec(memory_space=pltpu.HBM)
    sem = pltpu.SemaphoreType.DMA
    square = lambda *lead: pltpu.VMEM((*lead, N, N), F32)
    out = jax.ShapeDtypeStruct((HEADS, N, N), F32)
    grads = pl.pallas_call(
        kernel,
        out_shape=(pltpu.VMEM((HEADS, N, N), F32),) * 2,
        in_specs=[hbm] * 7,
        out_specs=(vmem, vmem),
        scratch_shapes=[
            pltpu.VMEM((HEADS, N, N), BF16),
            pltpu.VMEM((HEADS, N, N), BF16),
            pltpu.VMEM((HEADS, N, N), BF16),
            pltpu.VMEM((HEADS, N, N), BF16),
            square(HEADS),
            pltpu.VMEM((HEADS, N), F32),
            pltpu.VMEM((4, HEADS, N), F32),
            pltpu.VMEM((HEADS, 16, N), BF16),
            pltpu.VMEM((HEADS, N + 8, N), F32),
            square(HEADS),
            square(HEADS, 2, 2),
            square(HEADS, 2),
            square(SIDE, 2),
            square(SIDE, 2),
            square(2),
            square(SIDE - 1, 2),
            square(SIDE, 2),
            square(),
            square(SIDE),
            square(HEADS),
            square(HEADS),
            square(HEADS),
            square(HEADS),
            square(HEADS),
            square(HEADS),
            square(HEADS),
            square(HEADS),
            square(HEADS),
            square(HEADS),
            square(HEADS),
            square(HEADS),
            square(HEADS),
            pltpu.VMEM((HEADS, 3, 8, N), F32),
            pltpu.VMEM((SIDE, 3, 8, N), F32),
            pltpu.VMEM((2, 8 * SIDE, N), F32),
            pltpu.VMEM((SIDE, 8, N), F32),
            pltpu.VMEM((HEADS, 3, 8, N), F32),
            pltpu.VMEM((HEADS, 8, N), F32),
            pltpu.VMEM((HEADS, N + 8, N), F32),
            sem((7,)),
            sem, sem,
            sem((HEADS,)), sem((HEADS,)),
            sem((SIDE,)), sem((SIDE,)),
            sem((SIDE, 2)), sem((SIDE, 2)),
            sem((SIDE,)), sem((HEADS,)),
            sem((HEADS,)), sem((HEADS,)),
            sem((SIDE,)), sem((HEADS,)),
            sem((SIDE,)), sem((SIDE,)),
            sem, sem,
        ],
        compiler_params=pltpu.CompilerParams(
            collective_id=0, has_side_effects=True, vmem_limit_bytes=56 * 2**20
        ),
        name="delta_backward",
    )(queries, keys, values_in, out_grad, logged_keep_factor, beta, conv_weight)
    return pl.pallas_call(
        deliver,
        out_shape=(out, out),
        in_specs=[vmem] * 2,
        out_specs=(hbm, hbm),
        scratch_shapes=[sem((2, HEADS))],
        compiler_params=pltpu.CompilerParams(vmem_limit_bytes=8 * 2**20),
        name="deliver",
    )(*grads)


def solution(mesh):
    in_specs = (
        P("head", "ctx", None),
        P("head", "ctx", None),
        P("head", "ctx", None),
        P("head", "ctx", None),
        P("head", "ctx", None),
        P("head", "ctx"),
        P(None, "head", None),
    )
    out_specs = (P("head", "ctx", None), P("head", "ctx", None))
    return jax.shard_map(local, mesh=mesh, in_specs=in_specs, out_specs=out_specs, check_vma=False)
```
